128 devices in a mesh: bl: 8 (over x, core), ma: 16 (over z, y).
Axes of the slice: x: 4, y: 4, z: 4, core: 2. Of those that a mesh axis runs over, the one named last changes fastest.
Arguments:
- beam_fringe_harmonics: bfloat16 [128, 32, 2, 1024], P('bl'), may hold values from -6 to 6
- legendre: bfloat16 [32, 1536, 1024], P(None, 'ma'), may hold values from -0.1875 to 0.1875
- visibility: float32 [128, 2, 4096], P('bl', None, 'ma'), may hold values from -6 to 6
- owner_orders: int32 [16, 4], replicated, may hold values from 0 to 32, as said below
Outputs:
- normal: bfloat16 [64, 2, 1536, 1536], P('ma', None, 'bl')
- dirty_map: float32 [64, 2, 1536], P('ma', None, 'bl')
The draws below stay inside these ranges and needn't reach their ends.
Inputs may be any that keep to these rules, and one draw needn't show every extreme that they name: `owner_orders`: row k lists the orders that owner k holds in its first slots; each of the 32 orders stands in exactly one slot and the other slots hold 32. Owners hold from 0 to 4 orders, and in every draw some owner holds 4 and some none.
All inputs are finite; a program needn't handle non-finite values.
Results may differ from the reference program's by a relative error of at most 0.0056.
Values may be sent and summed in bfloat16 or wider, within the bound.
A program may use at most 64 MiB of HBM per device.

```python
import math
import jax
import jax.numpy as jnp
from jax import lax

L = 1536
NTH = 1024
NT = 4096
NB = 128
M = 32
CAP = 4
SLOTS = 64


def draw_owner_orders(key, part):
    key = jax.random.fold_in(key, 11)
    key_first, key_forced, key_shuffle = jax.random.split(key, 3)
    owner_count = SLOTS // CAP
    pair_count = owner_count // 2
    first_counts = jax.random.randint(key_first, (pair_count,), 0, CAP + 1)
    forced_pair = jax.random.randint(key_forced, (), 0, pair_count)
    first_counts = jnp.where(jnp.arange(pair_count) == forced_pair, CAP, first_counts)
    counts = jnp.stack([first_counts, CAP - first_counts], axis=1).reshape(owner_count)
    offsets = jnp.cumsum(counts) - counts
    shuffled = jax.random.permutation(key_shuffle, M).astype(jnp.int32)
    positions = jnp.arange(CAP)
    indices = jnp.minimum(offsets[:, None] + positions[None, :], M - 1)
    filled = positions[None, :] < counts[:, None]
    return jnp.where(filled, shuffled[indices], M).astype(jnp.int32)


def block_levels(stream_key, extent, pieces, smallest, largest):
    def one(position, blocks):
        heights = jax.random.uniform(jax.random.fold_in(jax.random.fold_in(stream_key, 6), position), (blocks,), jnp.float32, smallest / len(pieces), largest / len(pieces))
        return jnp.repeat(jnp.exp(heights), extent[position] // blocks).reshape((-1,) + (1,) * (len(extent) - position - 1))

    gain = one(*pieces[0])
    for cut in pieces[1:]:
        gain = gain * one(*cut)
    return gain


def gaussian(rng, dims, width, limit, cuts=(), held_as=jnp.bfloat16):
    loudness = block_levels(rng, dims, cuts, -0.22, 0.18) if cuts else 1.0
    entries = jax.random.normal(rng, dims, jnp.float32) * width * loudness
    return jnp.minimum(jnp.maximum(entries, -limit), limit).astype(held_as)


def setup_inputs(seed: int = 0) -> dict:
    streams_of = jax.random.split(jax.random.key(seed), 5)
    return {
        "beam_fringe_harmonics": gaussian(streams_of[0], (NB, M, 2, NTH), 1.0, 6.0, ((0, 8),)),
        "legendre": gaussian(streams_of[1], (M, L, NTH), NTH ** -0.5, 0.1875, ((1, 16),)),
        "visibility": gaussian(streams_of[2], (NB, 2, NT), 1.0, 6.0, ((0, 8), (2, 16)), jnp.float32),
        "owner_orders": draw_owner_orders(jax.random.fold_in(streams_of[4], 71), 0),
    }


def reference(beam_fringe_harmonics, legendre, visibility, owner_orders):
    harmonic = jnp.einsum('bmct,mlt->mbcl', beam_fringe_harmonics.astype(jnp.float32), legendre.astype(jnp.float32), precision=lax.Precision.HIGHEST).astype(jnp.bfloat16)
    orders = owner_orders.reshape(-1)
    filled = orders < M
    clipped = jnp.minimum(orders, M - 1).astype(jnp.int32)
    blocks = jnp.where(filled[:, None, None, None], harmonic[clipped], jnp.zeros((), jnp.bfloat16))
    times = jnp.arange(NT, dtype=jnp.int32)
    phases = times[:, None] * clipped[None, :] % NT
    angles = phases.astype(jnp.float32) * (2.0 * math.pi / NT)
    cosine = jnp.cos(angles)
    sine_table = jnp.sin(angles)
    usable = filled.astype(jnp.float32) / math.sqrt(NT)
    real_in = visibility[:, 0, :]
    imag_in = visibility[:, 1, :]
    maximum_degree = lax.Precision.HIGHEST
    real_out = (jnp.dot(real_in, cosine, precision=maximum_degree) + jnp.dot(imag_in, sine_table, precision=maximum_degree)) * usable
    imag_out = (jnp.dot(imag_in, cosine, precision=maximum_degree) - jnp.dot(real_in, sine_table, precision=maximum_degree)) * usable
    spectra = jnp.stack([real_out, imag_out], axis=2).transpose(1, 0, 2).astype(jnp.bfloat16)

    def one_slot(pair):
        one_block, one_spectrum = pair
        block_wide = one_block.astype(jnp.float32)
        spectrum_wide = one_spectrum.astype(jnp.float32)
        real_part = jnp.einsum('bkr,bkc->rc', block_wide, block_wide, precision=maximum_degree)
        cross = jnp.einsum('br,bc->rc', block_wide[:, 0], block_wide[:, 1], precision=maximum_degree)
        imag_part = cross - cross.T
        normal_slot = (jnp.stack([real_part, imag_part]) / NB).astype(jnp.bfloat16)
        dirty_real = lax.optimization_barrier(jnp.sum(block_wide[:, 0] * spectrum_wide[:, 0:1] + block_wide[:, 1] * spectrum_wide[:, 1:2], axis=0))
        dirty_imag = lax.optimization_barrier(jnp.sum(block_wide[:, 0] * spectrum_wide[:, 1:2] - block_wide[:, 1] * spectrum_wide[:, 0:1], axis=0))
        return (normal_slot, jnp.stack([dirty_real, dirty_imag]) / math.sqrt(NB))
    normal, dirty_map = lax.map(one_slot, (blocks, spectra))
    return (normal, dirty_map)
```

```python
import functools
import math

import jax
import jax.numpy as jnp
from jax import lax
from jax.experimental import pallas as pl
from jax.experimental.pallas import tpu as pltpu
from jax.sharding import PartitionSpec as P

F32 = jnp.float32
BF16 = jnp.bfloat16
MESH = pl.DeviceIdType.MESH

NZ = 4
NY = 4
NX = 4
CAP = 4
ORDERS = 32
DEG = 96
PACK = 112
ROWS = 32
COLS = 1536
GROUP = 8
RELATIVE = (0, 1, 3, 2)


def gather_kernel(
    orders_ref, legendre_ref, beam_ref, visibility_ref,
    blocks_ref, spectra_ref,
    legendre, beam, harmonic, outgoing, arrived, held, spectra,
    load_sem, beam_sem, a_send, a_recv, x_send, x_recv, c_send, c_recv, s_send, s_recv, out_sem,
):
    bl = lax.axis_index("bl")
    ma = lax.axis_index("ma")
    x, core = bl // 2, bl % 2
    z, y = ma // NY, ma % NY
    right = ((x + 1) % NX) * 2 + core
    left = ((x + NX - 1) % NX) * 2 + core
    across = ((x + 2) % NX) * 2 + core
    sibling = x * 2 + (1 - core)

    beam_load = pltpu.make_async_copy(beam_ref, beam, beam_sem)
    beam_load.start()
    loads = []
    for g in range(ORDERS // GROUP):
        part = pl.ds(g * GROUP, GROUP)
        load = pltpu.make_async_copy(legendre_ref.at[part], legendre.at[part], load_sem.at[g])
        load.start()
        loads.append(load)

    barrier = pltpu.get_barrier_semaphore()
    for dz in range(NZ):
        for dy in range(NY):
            if dz or dy:
                peer = ((z + dz) % NZ) * NY + (y + dy) % NY
                pl.semaphore_signal(barrier, inc=1, device_id={"bl": bl, "ma": peer}, device_id_type=MESH)
    for d in range(1, 2 * NX):
        pl.semaphore_signal(
            barrier, inc=1, device_id={"bl": (bl + d) % (2 * NX), "ma": ma}, device_id_type=MESH
        )

    times = visibility_ref.shape[2]
    total_time = times * NZ * NY
    order_index = lax.broadcasted_iota(jnp.int32, (ORDERS, times), 0)
    time_index = lax.broadcasted_iota(jnp.int32, (ORDERS, times), 1) + ma * times
    angle = ((order_index * time_index) & (total_time - 1)).astype(F32) * (2.0 * math.pi / total_time)
    cosine, sine = jnp.cos(angle), jnp.sin(angle)
    real = visibility_ref[:, 0, :]
    imag = visibility_ref[:, 1, :]
    direct = jnp.concatenate([real, imag] * CAP, axis=0)
    turned = jnp.concatenate([imag, -real] * CAP, axis=0)
    contract = (((1,), (1,)), ((), ()))
    partial = (
        lax.dot_general(cosine, direct, contract, precision=lax.Precision.HIGHEST, preferred_element_type=F32)
        + lax.dot_general(sine, turned, contract, precision=lax.Precision.HIGHEST, preferred_element_type=F32)
    ) * (1.0 / math.sqrt(total_time))
    high = partial.astype(BF16).astype(F32)
    low = partial - high
    row = lax.broadcasted_iota(jnp.int32, (PACK - DEG, 128), 0)
    for m in range(ORDERS):
        harmonic[m, DEG:PACK, :] = jnp.where(
            row == 0, high[m : m + 1], jnp.where(row == 1, low[m : m + 1], 0.0)
        ).astype(BF16)
    harmonic[ORDERS] = jnp.zeros((PACK, 128), BF16)

    lane = lax.broadcasted_iota(jnp.int32, (DEG, 128), 1) // ROWS
    beam_load.wait()
    for g in range(ORDERS // GROUP):
        loads[g].wait()
        part = pl.ds(g * GROUP, GROUP)
        product = lax.dot_general(
            legendre[part].reshape(GROUP * DEG, -1),
            beam[part].reshape(GROUP * ROWS, -1),
            contract,
            preferred_element_type=F32,
        )
        for i in range(GROUP):
            half = (i * ROWS) // 128
            own = product[i * DEG : (i + 1) * DEG, half * 128 : (half + 1) * 128]
            own = jnp.where(lane == i % (128 // ROWS), own, 0.0)
            own = own + pltpu.roll(own, ROWS, 1)
            own = own + pltpu.roll(own, 2 * ROWS, 1)
            harmonic[g * GROUP + i, 0:DEG, :] = own.astype(BF16)

    pl.semaphore_wait(barrier, NZ * NY - 1 + 2 * NX - 1)

    slot_lane = lax.broadcasted_iota(jnp.int32, (PACK, 128), 1) // ROWS
    exchange = []
    for t in range(NZ):
        for dy in range(NY):
            n = t * NY + dy
            owner = ((z + NZ - RELATIVE[t]) % NZ) * NY + (y + dy) % NY
            parts = [harmonic[orders_ref[owner * CAP + s]] for s in range(CAP)]
            block = jnp.where(
                slot_lane < 2,
                jnp.where(slot_lane == 0, parts[0], parts[1]),
                jnp.where(slot_lane == 2, parts[2], parts[3]),
            )
            if n == 0:
                arrived[ma] = block
                exchange.append(None)
            else:
                outgoing[n] = block
                copy = pltpu.make_async_remote_copy(
                    src_ref=outgoing.at[n],
                    dst_ref=arrived.at[ma],
                    send_sem=a_send.at[n],
                    recv_sem=a_recv.at[n],
                    device_id={"bl": bl, "ma": owner},
                    device_id_type=MESH,
                )
                copy.start()
                exchange.append(copy)

    sent = []

    def view(t, who, first=0, count=ROWS):
        zs = (z + RELATIVE[t]) % NZ
        start = pl.multiple_of(who * ROWS + first, 16)
        return held.at[:, pl.ds(start, count), pl.ds(pl.multiple_of(zs * (NY * DEG), 128), NY * DEG)]

    def send(ref, to, send_sem, recv_sem):
        copy = pltpu.make_async_remote_copy(
            src_ref=ref, dst_ref=ref, send_sem=send_sem, recv_sem=recv_sem,
            device_id={"bl": to, "ma": ma}, device_id_type=MESH,
        )
        copy.start()
        sent.append(copy)

    def await_view(ref, recv_sem):
        pltpu.make_async_copy(ref, ref, recv_sem).wait()

    def own_part(t):
        for dy in range(NY):
            if t or dy:
                exchange[t * NY + dy].wait_recv()
        zs = (z + RELATIVE[t]) % NZ
        stacked = jnp.concatenate([arrived[zs * NY + j, 0:DEG, :] for j in range(NY)], axis=0)
        held[:, pl.ds(pl.multiple_of(bl * ROWS, 16), ROWS),
             pl.ds(pl.multiple_of(zs * (NY * DEG), 128), NY * DEG)] = stacked.T.reshape(CAP, ROWS, NY * DEG)
        send(view(t, bl), right, x_send.at[t, 0], x_recv.at[t, 0])
        send(view(t, bl), left, x_send.at[t, 1], x_recv.at[t, 1])
        send(view(t, bl), sibling, c_send.at[t, 0], c_recv.at[t, 0])

    def near_part(t):
        await_view(view(t, left), x_recv.at[t, 0])
        send(view(t, left, 0, ROWS // 2), right, x_send.at[t, 2], x_recv.at[t, 2])
        send(view(t, left), sibling, c_send.at[t, 1], c_recv.at[t, 1])
        await_view(view(t, right), x_recv.at[t, 1])
        send(view(t, right, ROWS // 2, ROWS // 2), left, x_send.at[t, 3], x_recv.at[t, 3])
        send(view(t, right), sibling, c_send.at[t, 2], c_recv.at[t, 2])

    def far_part(t):
        await_view(view(t, across, 0, ROWS // 2), x_recv.at[t, 2])
        await_view(view(t, across, ROWS // 2, ROWS // 2), x_recv.at[t, 3])
        send(view(t, across), sibling, c_send.at[t, 3], c_recv.at[t, 3])

    own_part(0)
    own_part(1)
    near_part(0)
    own_part(2)
    near_part(1)
    far_part(0)
    own_part(3)

    total = jnp.zeros((PACK - DEG, 128), F32)
    for k in range(NZ * NY):
        total = total + arrived[k, DEG:PACK, :].astype(F32)
    line = jnp.sum(total, axis=0, keepdims=True).astype(BF16).astype(F32)
    spectra[bl] = jnp.broadcast_to(line, (8, 128))
    spectra_sent = []
    for d in range(1, 2 * NX):
        copy = pltpu.make_async_remote_copy(
            src_ref=spectra.at[bl], dst_ref=spectra.at[bl], send_sem=s_send.at[d], recv_sem=s_recv.at[d],
            device_id={"bl": (bl + d) % (2 * NX), "ma": ma}, device_id_type=MESH,
        )
        copy.start()
        spectra_sent.append(copy)

    near_part(2)
    far_part(1)
    near_part(3)
    far_part(2)
    far_part(3)

    other = 1 - 2 * core
    for t in range(NZ):
        await_view(view(t, bl + other), c_recv.at[t, 0])
        await_view(view(t, left + other), c_recv.at[t, 1])
        await_view(view(t, right + other), c_recv.at[t, 2])
        await_view(view(t, across + other), c_recv.at[t, 3])
    for d in range(1, 2 * NX):
        spectra_sent[d - 1].wait_recv()
    out = pltpu.make_async_copy(held, blocks_ref, out_sem.at[0])
    out.start()
    out2 = pltpu.make_async_copy(spectra, spectra_ref, out_sem.at[1])
    out2.start()
    for copy in exchange[1:]:
        copy.wait_send()
    for copy in sent + spectra_sent:
        copy.wait_send()
    out.wait()
    out2.wait()


def gather(orders, legendre, beam, visibility):
    any_spec = pl.BlockSpec(memory_space=pl.ANY)
    dma = pltpu.SemaphoreType.DMA
    return pl.pallas_call(
        gather_kernel,
        out_shape=(
            jax.ShapeDtypeStruct((CAP, 2 * NX * ROWS, COLS), BF16),
            jax.ShapeDtypeStruct((2 * NX, 8, 128), F32),
        ),
        in_specs=[
            pl.BlockSpec(memory_space=pltpu.SMEM),
            any_spec,
            any_spec,
            pl.BlockSpec(memory_space=pltpu.VMEM),
        ],
        out_specs=(any_spec, any_spec),
        scratch_shapes=[
            pltpu.VMEM(legendre.shape, BF16),
            pltpu.VMEM(beam.shape, BF16),
            pltpu.VMEM((ORDERS + 1, PACK, 128), BF16),
            pltpu.VMEM((NZ * NY, PACK, 128), BF16),
            pltpu.VMEM((NZ * NY, PACK, 128), BF16),
            pltpu.VMEM((CAP, 2 * NX * ROWS, COLS), BF16),
            pltpu.VMEM((2 * NX, 8, 128), F32),
            dma((ORDERS // GROUP,)),
            dma,
            dma((NZ * NY,)),
            dma((NZ * NY,)),
            dma((NZ, 4)),
            dma((NZ, 4)),
            dma((NZ, 4)),
            dma((NZ, 4)),
            dma((2 * NX,)),
            dma((2 * NX,)),
            dma((2,)),
        ],
        compiler_params=pltpu.CompilerParams(
            collective_id=0, has_side_effects=True, vmem_limit_bytes=40 * 1024 * 1024
        ),
        name="gather_blocks",
    )(orders, legendre, beam, visibility)


def normal_kernel(blocks_ref, spectra_ref, normal_ref, map_ref, turned, own):
    s = pl.program_id(0)
    bl = lax.axis_index("bl")
    start = pl.multiple_of(((3 * bl) // 2) * 128, 128)
    skip = pl.multiple_of((bl % 2) * 64, 16)
    window = blocks_ref[0, :, pl.ds(start, 256)]
    pieces = []
    for k in range(2 * NX):
        pieces.append(-window[k * ROWS + ROWS // 2 : (k + 1) * ROWS])
        pieces.append(window[k * ROWS : k * ROWS + ROWS // 2])
    own[...] = window.T
    turned[...] = jnp.concatenate(pieces, axis=0).T
    left = jnp.concatenate([own[pl.ds(skip, 192), :], turned[pl.ds(skip, 192), :]], axis=0)
    scale = 1.0 / 128.0
    for n in range(COLS // 256):
        part = pl.ds(n * 256, 256)
        product = jnp.dot(left, blocks_ref[0, :, part], preferred_element_type=F32) * scale
        normal_ref[0, 0, :, part] = product[0:192].astype(BF16)
        normal_ref[0, 1, :, part] = product[192:384].astype(BF16)
    lane = lax.broadcasted_iota(jnp.int32, (8, 128), 1) // ROWS
    halves = []
    for h in range(2):
        line = jnp.zeros((8, 128), F32)
        for q in range(4):
            moved = pltpu.roll(spectra_ref[h * 4 + q], (q * ROWS + 128 - s * ROWS) % 128, 1)
            line = jnp.where(lane == q, moved, line)
        halves.append(line)
    spectrum = jnp.concatenate(halves, axis=1).astype(BF16)
    adjoint = lax.dot_general(spectrum, left, (((1,), (1,)), ((), ())), preferred_element_type=F32)
    adjoint = adjoint * (1.0 / math.sqrt(128.0))
    map_ref[0, 0:1, :] = adjoint[0:1, 0:192]
    map_ref[0, 1:2, :] = adjoint[0:1, 192:384]


def normal_maps(blocks, spectra):
    return pl.pallas_call(
        normal_kernel,
        grid=(CAP,),
        out_shape=(
            jax.ShapeDtypeStruct((CAP, 2, 192, COLS), BF16),
            jax.ShapeDtypeStruct((CAP, 2, 192), F32),
        ),
        in_specs=[
            pl.BlockSpec((1, 256, COLS), lambda s: (s, 0, 0)),
            pl.BlockSpec((2 * NX, 8, 128), lambda s: (0, 0, 0)),
        ],
        out_specs=(
            pl.BlockSpec((1, 2, 192, COLS), lambda s: (s, 0, 0, 0)),
            pl.BlockSpec((1, 2, 192), lambda s: (s, 0, 0)),
        ),
        scratch_shapes=[pltpu.VMEM((256, 256), BF16), pltpu.VMEM((256, 256), BF16)],
        compiler_params=pltpu.CompilerParams(vmem_limit_bytes=40 * 1024 * 1024),
        name="normal_maps",
    )(blocks, spectra)


def on_device(beam_fringe_harmonics, legendre, visibility, owner_orders):
    beam = beam_fringe_harmonics.transpose(1, 2, 0, 3).reshape(ORDERS, ROWS, -1)
    blocks, spectra = gather(owner_orders.reshape(-1), legendre, beam, visibility)
    return normal_maps(blocks, spectra)


def solution(mesh):
    return jax.shard_map(
        on_device,
        mesh=mesh,
        in_specs=(P("bl", None, None, None), P(None, "ma", None), P("bl", None, "ma"), P()),
        out_specs=(P("ma", None, "bl", None), P("ma", None, "bl")),
        check_vma=False,
    )
```

```python
import functools
import math

import jax
import jax.numpy as jnp
from jax import lax
from jax.experimental import pallas as pl
from jax.experimental.pallas import tpu as pltpu
from jax.sharding import PartitionSpec as P

F32 = jnp.float32
BF16 = jnp.bfloat16
MESH = pl.DeviceIdType.MESH

NZ = 4
NY = 4
NX = 4
CAP = 4
ORDERS = 32
DEG = 96
PACK = 112
ROWS = 32
COLS = 1536
GROUP = 8
RELATIVE = (0, 1, 3, 2)


def gather_kernel(
    orders_ref, legendre_ref, beam_ref, visibility_ref,
    held, spectra,
    orders, legendre, beam, visibility, rows, products, harmonic, outgoing, arrived,
    load_sem, beam_sem, a_send, a_recv, x_send, x_recv, c_send, c_recv, s_send, s_recv,
):
    bl = lax.axis_index("bl")
    ma = lax.axis_index("ma")
    x, core = bl // 2, bl % 2
    z, y = ma // NY, ma % NY
    right = ((x + 1) % NX) * 2 + core
    left = ((x + NX - 1) % NX) * 2 + core
    across = ((x + 2) % NX) * 2 + core
    sibling = x * 2 + (1 - core)

    visibility_load = pltpu.make_async_copy(visibility_ref, visibility, beam_sem.at[0])
    visibility_load.start()
    beam_load = pltpu.make_async_copy(beam_ref, beam, beam_sem.at[1])
    beam_load.start()
    loads = []
    for g in range(ORDERS // GROUP):
        part = pl.ds(g * GROUP, GROUP)
        load = pltpu.make_async_copy(legendre_ref.at[part], legendre.at[part], load_sem.at[g])
        load.start()
        loads.append(load)
    orders_load = pltpu.make_async_copy(orders_ref, orders, beam_sem.at[2])
    orders_load.start()

    barrier = pltpu.get_barrier_semaphore()
    for d in range(1, NZ * NY):
        peer = ((z + d // NY) % NZ) * NY + (y + d) % NY
        pl.semaphore_signal(barrier, inc=1, device_id={"bl": bl, "ma": peer}, device_id_type=MESH)
    for d in range(1, 2 * NX):
        peer = (bl + d) % (2 * NX)
        pl.semaphore_signal(barrier, inc=1, device_id={"bl": peer, "ma": ma}, device_id_type=MESH)

    times = visibility_ref.shape[2]
    total_time = times * NZ * NY
    order_index = lax.broadcasted_iota(jnp.int32, (ORDERS, times), 0)
    time_index = lax.broadcasted_iota(jnp.int32, (ORDERS, times), 1) + ma * times
    angle = ((order_index * time_index) & (total_time - 1)).astype(F32) * (2.0 * math.pi / total_time)
    cosine, sine = jnp.cos(angle), jnp.sin(angle)
    visibility_load.wait()
    real = visibility[:, 0, :]
    imag = visibility[:, 1, :]
    direct = jnp.concatenate([real, imag] * CAP, axis=0)
    turned = jnp.concatenate([imag, -real] * CAP, axis=0)
    contract = (((1,), (1,)), ((), ()))
    partial = (
        lax.dot_general(cosine, direct, contract, precision=lax.Precision.HIGHEST, preferred_element_type=F32)
        + lax.dot_general(sine, turned, contract, precision=lax.Precision.HIGHEST, preferred_element_type=F32)
    ) * (1.0 / math.sqrt(total_time))
    high = partial.astype(BF16).astype(F32)
    low = partial - high
    row = lax.broadcasted_iota(jnp.int32, (PACK - DEG, 128), 0)
    for m in range(ORDERS):
        harmonic[m, DEG:PACK, :] = jnp.where(
            row == 0, high[m : m + 1], jnp.where(row == 1, low[m : m + 1], 0.0)
        ).astype(BF16)
    harmonic[ORDERS] = jnp.zeros((PACK, 128), BF16)

    beam_load.wait()
    for g in range(ORDERS // GROUP):
        rows[g] = beam[:, g * GROUP : (g + 1) * GROUP].reshape(GROUP * ROWS, -1)
    part = GROUP // 2
    for g in range(ORDERS // GROUP):
        loads[g].wait()
        for first in range(0, GROUP, part):
            product = lax.dot_general(
                legendre[g * GROUP + first : g * GROUP + first + part].reshape(part * DEG, -1),
                rows[g],
                contract,
                preferred_element_type=F32,
            ).astype(BF16)
            for i in range(part):
                products[first + i, g * DEG : (g + 1) * DEG] = product[i * DEG : (i + 1) * DEG]
    source = lax.broadcasted_iota(jnp.int32, (GROUP * ROWS, 128), 0)
    column = lax.broadcasted_iota(jnp.int32, (GROUP * ROWS, 128), 1) % ROWS
    wanted = (column % (ROWS // 2)) * (2 * GROUP) + column // (ROWS // 2)
    for i in range(GROUP):
        pick = (source == wanted + 2 * i).astype(F32).astype(BF16)
        picked = jnp.dot(products[i], pick, preferred_element_type=F32).astype(BF16)
        for g in range(ORDERS // GROUP):
            harmonic[g * GROUP + i, 0:DEG, :] = picked[g * DEG : (g + 1) * DEG]
    orders_load.wait()

    pl.semaphore_wait(barrier, NZ * NY - 1 + 2 * NX - 1)

    slot_lane = lax.broadcasted_iota(jnp.int32, (PACK, 128), 1) // ROWS
    def to_owner(t, dy):
        n = t * NY + dy
        owner = ((z + NZ - RELATIVE[t]) % NZ) * NY + (y + dy) % NY
        parts = [harmonic[orders[s, owner]] for s in range(CAP)]
        block = jnp.where(
            slot_lane < 2,
            jnp.where(slot_lane == 0, parts[0], parts[1]),
            jnp.where(slot_lane == 2, parts[2], parts[3]),
        )
        if n == 0:
            arrived[ma] = block
            return
        outgoing[n] = block
        copy = pltpu.make_async_remote_copy(
            src_ref=outgoing.at[n],
            dst_ref=arrived.at[ma],
            send_sem=a_send,
            recv_sem=a_recv.at[t],
            device_id={"bl": bl, "ma": owner},
            device_id_type=MESH,
        )
        copy.start()

    for t in range(NZ):
        for dy in range(NY):
            to_owner(t, dy)

    def view(t, who, first=0, count=CAP):
        return held.at[(z + RELATIVE[t]) % NZ, who, pl.ds(first, count)]

    def send(ref, to, send_sem, recv_sem):
        copy = pltpu.make_async_remote_copy(
            src_ref=ref, dst_ref=ref, send_sem=send_sem, recv_sem=recv_sem,
            device_id={"bl": to, "ma": ma}, device_id_type=MESH,
        )
        copy.start()

    def await_bytes(ref, sem):
        pltpu.make_async_copy(ref, ref, sem).wait()

    def own_part(t):
        zs = (z + RELATIVE[t]) % NZ
        count = NY if t else NY - 1
        await_bytes(arrived.at[pl.ds(0, count)], a_recv.at[t])
        stacked = jnp.concatenate([arrived[zs * NY + j, 0:DEG, :] for j in range(NY)], axis=0)
        held[zs, bl] = stacked.T.reshape(CAP, ROWS, NY * DEG)
        send(view(t, bl), right, x_send, x_recv.at[t, 0])
        send(view(t, bl), left, x_send, x_recv.at[t, 1])
        send(view(t, bl), sibling, c_send, c_recv)

    def near_part(t):
        await_bytes(view(t, left), x_recv.at[t, 0])
        send(view(t, left, 0, CAP // 2), right, x_send, x_recv.at[t, 2])
        send(view(t, left), sibling, c_send, c_recv)
        await_bytes(view(t, right), x_recv.at[t, 1])
        send(view(t, right, CAP // 2, CAP // 2), left, x_send, x_recv.at[t, 2])
        send(view(t, right), sibling, c_send, c_recv)

    def far_part(t):
        await_bytes(view(t, across), x_recv.at[t, 2])
        send(view(t, across), sibling, c_send, c_recv)

    own_part(0)
    own_part(1)
    near_part(0)
    own_part(2)
    own_part(3)

    total = jnp.zeros((PACK - DEG, 128), F32)
    for k in range(NZ * NY):
        total = total + arrived[k, DEG:PACK, :].astype(F32)
    line = jnp.sum(total, axis=0, keepdims=True).astype(BF16).astype(F32)
    spectra[bl] = jnp.broadcast_to(line, (8, 128))
    for d in range(1, 2 * NX):
        copy = pltpu.make_async_remote_copy(
            src_ref=spectra.at[bl], dst_ref=spectra.at[bl], send_sem=s_send, recv_sem=s_recv,
            device_id={"bl": (bl + d) % (2 * NX), "ma": ma}, device_id_type=MESH,
        )
        copy.start()

    near_part(1)
    far_part(0)
    near_part(2)
    far_part(1)
    near_part(3)
    far_part(2)
    far_part(3)

    await_bytes(held.at[pl.ds(0, NZ // 2)], c_recv)
    await_bytes(spectra.at[pl.ds(0, 2 * NX - 1)], s_recv)
    await_bytes(outgoing.at[pl.ds(0, NZ * NY - 1)], a_send)
    await_bytes(held.at[pl.ds(0, NZ - 1), pl.ds(0, NX)], x_send)
    await_bytes(held.at[pl.ds(0, NZ // 2)], c_send)
    await_bytes(spectra.at[pl.ds(0, 2 * NX - 1)], s_send)


def gather(orders, legendre, beam, visibility):
    hbm = pl.BlockSpec(memory_space=pltpu.HBM)
    vmem = pl.BlockSpec(memory_space=pltpu.VMEM)
    dma = pltpu.SemaphoreType.DMA
    return pl.pallas_call(
        gather_kernel,
        out_shape=(
            jax.ShapeDtypeStruct((NZ, 2 * NX, CAP, ROWS, NY * DEG), BF16),
            jax.ShapeDtypeStruct((2 * NX, 8, 128), F32),
        ),
        in_specs=[
            hbm,
            hbm,
            hbm,
            hbm,
        ],
        out_specs=(vmem, vmem),
        scratch_shapes=[
            pltpu.SMEM(orders.shape, jnp.int32),
            pltpu.VMEM(legendre.shape, BF16),
            pltpu.VMEM(beam.shape, BF16),
            pltpu.VMEM(visibility.shape, F32),
            pltpu.VMEM((ORDERS // GROUP, GROUP * ROWS, beam.shape[3]), BF16),
            pltpu.VMEM((GROUP, ORDERS // GROUP * DEG, GROUP * ROWS), BF16),
            pltpu.VMEM((ORDERS + 1, PACK, 128), BF16),
            pltpu.VMEM((NZ * NY, PACK, 128), BF16),
            pltpu.VMEM((NZ * NY, PACK, 128), BF16),
            dma((ORDERS // GROUP,)),
            dma((3,)),
            dma,
            dma((NZ,)),
            dma,
            dma((NZ, 3)),
            dma,
            dma,
            dma,
            dma,
        ],
        compiler_params=pltpu.CompilerParams(
            collective_id=0, has_side_effects=True, vmem_limit_bytes=40 * 1024 * 1024
        ),
        name="gather_blocks",
    )(orders, legendre, beam, visibility)


def normal_kernel(blocks_ref, spectra_ref, normal_ref, map_ref, turned, own):
    s = pl.program_id(0)
    bl = lax.axis_index("bl")
    start = pl.multiple_of((bl % 2) * 128, 128)
    skip = pl.multiple_of((bl % 2) * 64, 16)
    window = blocks_ref[bl // 2, :, s, :, pl.ds(start, 256)].reshape(2 * NX * ROWS, 256)
    pieces = []
    for k in range(2 * NX):
        pieces.append(-window[k * ROWS + ROWS // 2 : (k + 1) * ROWS])
        pieces.append(window[k * ROWS : k * ROWS + ROWS // 2])
    own[...] = window.T
    turned[...] = jnp.concatenate(pieces, axis=0).T
    left = jnp.concatenate([own[pl.ds(skip, 192), :], turned[pl.ds(skip, 192), :]], axis=0)
    scale = 1.0 / 128.0
    width = NY * DEG
    for n in range(0, NZ, 2):
        right = jnp.concatenate(
            [blocks_ref[n + h, :, s].reshape(2 * NX * ROWS, width) for h in range(2)], axis=1
        )
        product = jnp.dot(left, right, preferred_element_type=F32) * scale
        part = pl.ds(n * width, 2 * width)
        normal_ref[0, 0, :, part] = product[0:192].astype(BF16)
        normal_ref[0, 1, :, part] = product[192:384].astype(BF16)
    lane = lax.broadcasted_iota(jnp.int32, (8, 128), 1) // ROWS
    halves = []
    for h in range(2):
        line = jnp.zeros((8, 128), F32)
        for q in range(4):
            moved = pltpu.roll(spectra_ref[h * 4 + q], (q * ROWS + 128 - s * ROWS) % 128, 1)
            line = jnp.where(lane == q, moved, line)
        halves.append(line)
    spectrum = jnp.concatenate(halves, axis=1).astype(BF16)
    adjoint = lax.dot_general(spectrum, left, (((1,), (1,)), ((), ())), preferred_element_type=F32)
    adjoint = adjoint * (1.0 / math.sqrt(128.0))
    map_ref[0, 0:1, :] = adjoint[0:1, 0:192]
    map_ref[0, 1:2, :] = adjoint[0:1, 192:384]


def normal_maps(blocks, spectra):
    return pl.pallas_call(
        normal_kernel,
        grid=(CAP,),
        out_shape=(
            jax.ShapeDtypeStruct((CAP, 2, 192, COLS), BF16),
            jax.ShapeDtypeStruct((CAP, 2, 192), F32),
        ),
        in_specs=[
            pl.BlockSpec(memory_space=pltpu.VMEM),
            pl.BlockSpec(memory_space=pltpu.VMEM),
        ],
        out_specs=(
            pl.BlockSpec((1, 2, 192, COLS), lambda s: (s, 0, 0, 0)),
            pl.BlockSpec((1, 2, 192), lambda s: (s, 0, 0)),
        ),
        scratch_shapes=[pltpu.VMEM((256, 256), BF16), pltpu.VMEM((256, 256), BF16)],
        compiler_params=pltpu.CompilerParams(vmem_limit_bytes=40 * 1024 * 1024),
        name="normal_maps",
    )(blocks, spectra)


def on_device(beam_fringe_harmonics, legendre, visibility, owner_orders):
    in_hbm = [
        pltpu.with_memory_space_constraint(a, pltpu.HBM)
        for a in (owner_orders.T, legendre, beam_fringe_harmonics, visibility)
    ]
    blocks, spectra = gather(*in_hbm)
    return normal_maps(blocks, spectra)


def solution(mesh):
    return jax.shard_map(
        on_device,
        mesh=mesh,
        in_specs=(P("bl", None, None, None), P(None, "ma", None), P("bl", None, "ma"), P()),
        out_specs=(P("ma", None, "bl", None), P("ma", None, "bl")),
        check_vma=False,
    )
```

```python
import functools
import math

import jax
import jax.numpy as jnp
from jax import lax
from jax.experimental import pallas as pl
from jax.experimental.pallas import tpu as pltpu
from jax.sharding import PartitionSpec as P

F32 = jnp.float32
BF16 = jnp.bfloat16
MESH = pl.DeviceIdType.MESH

NZ = 4
NY = 4
NX = 4
CAP = 4
ORDERS = 32
DEG = 96
PACK = 112
ROWS = 32
COLS = 1536
GROUP = 8


def gather_kernel(
    orders_ref, legendre_ref, beam_ref, visibility_ref,
    held, spectra,
    orders, legendre, beam, visibility, rows, products, harmonic, outgoing, arrived,
    crossed, lined,
    load_sem, beam_sem, a_send, a_recv, k_send, k_recv, l_send, l_recv, p_send, p_recv,
    x_send, x_recv, c_send, c_recv, s_send, s_recv,
):
    bl = lax.axis_index("bl")
    ma = lax.axis_index("ma")
    x, core = bl // 2, bl % 2
    z, y = ma // NY, ma % NY
    right = ((x + 1) % NX) * 2 + core
    left = ((x + NX - 1) % NX) * 2 + core
    across = ((x + 2) % NX) * 2 + core
    sibling = x * 2 + (1 - core)

    visibility_load = pltpu.make_async_copy(visibility_ref, visibility, beam_sem.at[0])
    visibility_load.start()
    beam_load = pltpu.make_async_copy(beam_ref, beam, beam_sem.at[1])
    beam_load.start()
    loads = []
    for g in range(ORDERS // GROUP):
        part = pl.ds(g * GROUP, GROUP)
        load = pltpu.make_async_copy(legendre_ref.at[part], legendre.at[part], load_sem.at[g])
        load.start()
        loads.append(load)
    orders_load = pltpu.make_async_copy(orders_ref, orders, beam_sem.at[2])
    orders_load.start()

    barrier = pltpu.get_barrier_semaphore()
    for d in range(1, NZ * NY):
        peer = ((z + d // NY) % NZ) * NY + (y + d) % NY
        pl.semaphore_signal(barrier, inc=1, device_id={"bl": bl, "ma": peer}, device_id_type=MESH)
    for d in range(1, 2 * NX):
        peer = (bl + d) % (2 * NX)
        pl.semaphore_signal(barrier, inc=1, device_id={"bl": peer, "ma": ma}, device_id_type=MESH)

    times = visibility_ref.shape[2]
    total_time = times * NZ * NY
    order_index = lax.broadcasted_iota(jnp.int32, (ORDERS, times), 0)
    time_index = lax.broadcasted_iota(jnp.int32, (ORDERS, times), 1) + ma * times
    angle = ((order_index * time_index) & (total_time - 1)).astype(F32) * (2.0 * math.pi / total_time)
    cosine, sine = jnp.cos(angle), jnp.sin(angle)
    visibility_load.wait()
    real = visibility[:, 0, :]
    imag = visibility[:, 1, :]
    direct = jnp.concatenate([real, imag] * CAP, axis=0)
    turned = jnp.concatenate([imag, -real] * CAP, axis=0)
    contract = (((1,), (1,)), ((), ()))
    partial = (
        lax.dot_general(cosine, direct, contract, precision=lax.Precision.HIGHEST, preferred_element_type=F32)
        + lax.dot_general(sine, turned, contract, precision=lax.Precision.HIGHEST, preferred_element_type=F32)
    ) * (1.0 / math.sqrt(total_time))
    high = partial.astype(BF16).astype(F32)
    low = partial - high
    row = lax.broadcasted_iota(jnp.int32, (PACK - DEG, 128), 0)
    for m in range(ORDERS):
        harmonic[m, DEG:PACK, :] = jnp.where(
            row == 0, high[m : m + 1], jnp.where(row == 1, low[m : m + 1], 0.0)
        ).astype(BF16)
    harmonic[ORDERS] = jnp.zeros((PACK, 128), BF16)

    beam_load.wait()
    for g in range(ORDERS // GROUP):
        rows[g] = beam[:, g * GROUP : (g + 1) * GROUP].reshape(GROUP * ROWS, -1)
    part = GROUP // 2
    for g in range(ORDERS // GROUP):
        loads[g].wait()
        for first in range(0, GROUP, part):
            product = lax.dot_general(
                legendre[g * GROUP + first : g * GROUP + first + part].reshape(part * DEG, -1),
                rows[g],
                contract,
                preferred_element_type=F32,
            ).astype(BF16)
            for i in range(part):
                products[first + i, g * DEG : (g + 1) * DEG] = product[i * DEG : (i + 1) * DEG]
    source = lax.broadcasted_iota(jnp.int32, (GROUP * ROWS, 128), 0)
    column = lax.broadcasted_iota(jnp.int32, (GROUP * ROWS, 128), 1) % ROWS
    wanted = (column % (ROWS // 2)) * (2 * GROUP) + column // (ROWS // 2)
    for i in range(GROUP):
        pick = (source == wanted + 2 * i).astype(F32).astype(BF16)
        picked = jnp.dot(products[i], pick, preferred_element_type=F32).astype(BF16)
        for g in range(ORDERS // GROUP):
            harmonic[g * GROUP + i, 0:DEG, :] = picked[g * DEG : (g + 1) * DEG]
    orders_load.wait()

    pl.semaphore_wait(barrier, NZ * NY - 1 + 2 * NX - 1)

    def row(t, at_y):
        sign = 1 - 2 * (at_y % 2)
        return (0, sign, -sign, 2)[t]

    def owner_at(t, dy):
        at_y = (y + dy) % NY
        return (z + NZ - row(t, at_y)) % NZ, at_y

    slot_lane = lax.broadcasted_iota(jnp.int32, (PACK, 128), 1) // ROWS

    def block_for(at_z, at_y):
        owner = at_z * NY + at_y
        parts = [harmonic[orders[s, owner]] for s in range(CAP)]
        return jnp.where(
            slot_lane < 2,
            jnp.where(slot_lane == 0, parts[0], parts[1]),
            jnp.where(slot_lane == 2, parts[2], parts[3]),
        )

    def send(source, target, send_sem, recv_sem, to_bl, to_ma):
        pltpu.make_async_remote_copy(
            src_ref=source, dst_ref=target, send_sem=send_sem, recv_sem=recv_sem,
            device_id={"bl": to_bl, "ma": to_ma}, device_id_type=MESH,
        ).start()

    def await_bytes(ref, sem):
        pltpu.make_async_copy(ref, ref, sem).wait()

    for t in (1, 0):
        for dy in range(NY):
            at_z, at_y = owner_at(t, dy)
            block = block_for(at_z, at_y)
            crossed[x, t, at_y] = block[0:DEG]
            if t or dy:
                outgoing[t * NY + dy, DEG:PACK] = block[DEG:PACK]
            else:
                arrived[ma, DEG:PACK] = block[DEG:PACK]
        ref = crossed.at[x, t]
        send(ref, ref, k_send, k_recv.at[t, 0], right, ma)
        send(ref, ref, k_send, k_recv.at[t, 1], left, ma)

    for t in (2, 3):
        for dy in range(NY):
            at_z, at_y = owner_at(t, dy)
            n = t * NY + dy
            outgoing[n] = block_for(at_z, at_y)
            send(outgoing.at[n], arrived.at[ma], a_send, a_recv.at[t - 2], bl, at_z * NY + at_y)

    def pass_on(t, n, who):
        for dy in range(NY):
            if t or dy:
                at_z, at_y = owner_at(t, dy)
                send(crossed.at[who // 2, t, at_y], lined.at[t, who // 2, y],
                     l_send.at[t], l_recv.at[t, n], bl, at_z * NY + at_y)

    pass_on(1, 0, bl)
    pass_on(0, 0, bl)
    for t in (1, 0):
        for dy in range(NY):
            if t or dy:
                at_z, at_y = owner_at(t, dy)
                send(outgoing.at[t * NY + dy, pl.ds(DEG, PACK - DEG)], arrived.at[ma, pl.ds(DEG, PACK - DEG)],
                     p_send, p_recv, bl, at_z * NY + at_y)

    def cross_near(t):
        ref = crossed.at[left // 2, t]
        await_bytes(ref, k_recv.at[t, 0])
        half = crossed.at[left // 2, t, pl.ds(0, NY // 2)]
        send(half, half, k_send, k_recv.at[t, 2], right, ma)
        pass_on(t, 1, left)
        ref = crossed.at[right // 2, t]
        await_bytes(ref, k_recv.at[t, 1])
        half = crossed.at[right // 2, t, pl.ds(NY // 2, NY // 2)]
        send(half, half, k_send, k_recv.at[t, 2], left, ma)
        pass_on(t, 2, right)

    def cross_far(t):
        await_bytes(crossed.at[across // 2, t], k_recv.at[t, 2])
        pass_on(t, 3, across)

    def view(t, who, first=0, count=CAP):
        return held.at[(z + NZ + row(t, y)) % NZ, who, pl.ds(first, count)]

    def to_sibling(t, who):
        ref = view(t, who)
        send(ref, ref, c_send, c_recv, sibling, ma)

    def keep(t, who, blocks):
        stacked = jnp.concatenate(blocks, axis=0)
        held[(z + NZ + row(t, y)) % NZ, who] = stacked.T.reshape(CAP, ROWS, NY * DEG)

    def collect(t, n, who):
        await_bytes(lined.at[t, 0, pl.ds(0, NY if t else NY - 1)], l_recv.at[t, n])
        if t == 0:
            lined[t, who // 2, y] = crossed[who // 2, t, y]
        keep(t, who, [lined[t, who // 2, j] for j in range(NY)])
        to_sibling(t, who)

    def own_part(t):
        await_bytes(arrived.at[pl.ds(0, NY)], a_recv.at[t - 2])
        at_z = (z + NZ + row(t, y)) % NZ
        keep(t, bl, [arrived[at_z * NY + j, 0:DEG, :] for j in range(NY)])
        ref = view(t, bl)
        send(ref, ref, x_send, x_recv.at[t - 2, 0], right, ma)
        send(ref, ref, x_send, x_recv.at[t - 2, 1], left, ma)
        to_sibling(t, bl)

    def near_part(t):
        await_bytes(view(t, left), x_recv.at[t - 2, 0])
        ref = view(t, left, 0, CAP // 2)
        send(ref, ref, x_send, x_recv.at[t - 2, 2], right, ma)
        to_sibling(t, left)
        await_bytes(view(t, right), x_recv.at[t - 2, 1])
        ref = view(t, right, CAP // 2, CAP // 2)
        send(ref, ref, x_send, x_recv.at[t - 2, 2], left, ma)
        to_sibling(t, right)

    def far_part(t):
        await_bytes(view(t, across), x_recv.at[t - 2, 2])
        to_sibling(t, across)

    cross_near(1)
    cross_near(0)
    own_part(2)
    own_part(3)
    cross_far(1)
    cross_far(0)
    collect(1, 0, bl)
    collect(0, 0, bl)

    await_bytes(arrived.at[pl.ds(0, 2 * NY - 1), pl.ds(DEG, PACK - DEG)], p_recv)
    total = jnp.zeros((PACK - DEG, 128), F32)
    for k in range(NZ * NY):
        total = total + arrived[k, DEG:PACK, :].astype(F32)
    line = jnp.sum(total, axis=0, keepdims=True).astype(BF16).astype(F32)
    spectra[bl] = jnp.broadcast_to(line, (8, 128))
    for d in range(1, 2 * NX):
        send(spectra.at[bl], spectra.at[bl], s_send, s_recv, (bl + d) % (2 * NX), ma)

    collect(1, 1, left)
    collect(1, 2, right)
    collect(0, 1, left)
    collect(0, 2, right)
    near_part(2)
    near_part(3)
    collect(1, 3, across)
    collect(0, 3, across)
    far_part(2)
    far_part(3)

    await_bytes(held.at[pl.ds(0, NZ // 2)], c_recv)
    await_bytes(spectra.at[pl.ds(0, 2 * NX - 1)], s_recv)
    await_bytes(crossed.at[pl.ds(0, NX - 1)], k_send)
    await_bytes(outgoing.at[pl.ds(0, 2 * NY)], a_send)
    await_bytes(outgoing.at[pl.ds(0, 2 * NY - 1), pl.ds(DEG, PACK - DEG)], p_send)
    await_bytes(crossed.at[pl.ds(0, NX - 1), 0], l_send.at[0])
    await_bytes(crossed.at[:, 1], l_send.at[1])
    await_bytes(held.at[0, pl.ds(0, NX + 2)], x_send)
    await_bytes(held.at[pl.ds(0, NZ // 2)], c_send)
    await_bytes(spectra.at[pl.ds(0, 2 * NX - 1)], s_send)


def gather(orders, legendre, beam, visibility):
    hbm = pl.BlockSpec(memory_space=pltpu.HBM)
    vmem = pl.BlockSpec(memory_space=pltpu.VMEM)
    dma = pltpu.SemaphoreType.DMA
    return pl.pallas_call(
        gather_kernel,
        out_shape=(
            jax.ShapeDtypeStruct((NZ, 2 * NX, CAP, ROWS, NY * DEG), BF16),
            jax.ShapeDtypeStruct((2 * NX, 8, 128), F32),
        ),
        in_specs=[
            hbm,
            hbm,
            hbm,
            hbm,
        ],
        out_specs=(vmem, vmem),
        scratch_shapes=[
            pltpu.SMEM(orders.shape, jnp.int32),
            pltpu.VMEM(legendre.shape, BF16),
            pltpu.VMEM(beam.shape, BF16),
            pltpu.VMEM(visibility.shape, F32),
            pltpu.VMEM((ORDERS // GROUP, GROUP * ROWS, beam.shape[3]), BF16),
            pltpu.VMEM((GROUP, ORDERS // GROUP * DEG, GROUP * ROWS), BF16),
            pltpu.VMEM((ORDERS + 1, PACK, 128), BF16),
            pltpu.VMEM((NZ * NY, PACK, 128), BF16),
            pltpu.VMEM((NZ * NY, PACK, 128), BF16),
            pltpu.VMEM((NX, 2, NY, DEG, 128), BF16),
            pltpu.VMEM((2, NX, NY, DEG, 128), BF16),
            dma((ORDERS // GROUP,)),
            dma((3,)),
            dma,
            dma((2,)),
            dma,
            dma((2, 3)),
            dma((2,)),
            dma((2, 4)),
            dma,
            dma,
            dma,
            dma((2, 3)),
            dma,
            dma,
            dma,
            dma,
        ],
        compiler_params=pltpu.CompilerParams(
            collective_id=0, has_side_effects=True, vmem_limit_bytes=40 * 1024 * 1024
        ),
        name="gather_blocks",
    )(orders, legendre, beam, visibility)


def normal_kernel(blocks_ref, spectra_ref, normal_ref, map_ref, turned, own):
    s = pl.program_id(0)
    bl = lax.axis_index("bl")
    start = pl.multiple_of((bl % 2) * 128, 128)
    skip = pl.multiple_of((bl % 2) * 64, 16)
    window = blocks_ref[bl // 2, :, s, :, pl.ds(start, 256)].reshape(2 * NX * ROWS, 256)
    pieces = []
    for k in range(2 * NX):
        pieces.append(-window[k * ROWS + ROWS // 2 : (k + 1) * ROWS])
        pieces.append(window[k * ROWS : k * ROWS + ROWS // 2])
    own[...] = window.T
    turned[...] = jnp.concatenate(pieces, axis=0).T
    left = jnp.concatenate([own[pl.ds(skip, 192), :], turned[pl.ds(skip, 192), :]], axis=0)
    scale = 1.0 / 128.0
    width = NY * DEG
    for n in range(0, NZ, 2):
        right = jnp.concatenate(
            [blocks_ref[n + h, :, s].reshape(2 * NX * ROWS, width) for h in range(2)], axis=1
        )
        product = jnp.dot(left, right, preferred_element_type=F32) * scale
        part = pl.ds(n * width, 2 * width)
        normal_ref[0, 0, :, part] = product[0:192].astype(BF16)
        normal_ref[0, 1, :, part] = product[192:384].astype(BF16)
    lane = lax.broadcasted_iota(jnp.int32, (8, 128), 1) // ROWS
    halves = []
    for h in range(2):
        line = jnp.zeros((8, 128), F32)
        for q in range(4):
            moved = pltpu.roll(spectra_ref[h * 4 + q], (q * ROWS + 128 - s * ROWS) % 128, 1)
            line = jnp.where(lane == q, moved, line)
        halves.append(line)
    spectrum = jnp.concatenate(halves, axis=1).astype(BF16)
    adjoint = lax.dot_general(spectrum, left, (((1,), (1,)), ((), ())), preferred_element_type=F32)
    adjoint = adjoint * (1.0 / math.sqrt(128.0))
    map_ref[0, 0:1, :] = adjoint[0:1, 0:192]
    map_ref[0, 1:2, :] = adjoint[0:1, 192:384]


def normal_maps(blocks, spectra):
    return pl.pallas_call(
        normal_kernel,
        grid=(CAP,),
        out_shape=(
            jax.ShapeDtypeStruct((CAP, 2, 192, COLS), BF16),
            jax.ShapeDtypeStruct((CAP, 2, 192), F32),
        ),
        in_specs=[
            pl.BlockSpec(memory_space=pltpu.VMEM),
            pl.BlockSpec(memory_space=pltpu.VMEM),
        ],
        out_specs=(
            pl.BlockSpec((1, 2, 192, COLS), lambda s: (s, 0, 0, 0)),
            pl.BlockSpec((1, 2, 192), lambda s: (s, 0, 0)),
        ),
        scratch_shapes=[pltpu.VMEM((256, 256), BF16), pltpu.VMEM((256, 256), BF16)],
        compiler_params=pltpu.CompilerParams(vmem_limit_bytes=40 * 1024 * 1024),
        name="normal_maps",
    )(blocks, spectra)


def on_device(beam_fringe_harmonics, legendre, visibility, owner_orders):
    in_hbm = [
        pltpu.with_memory_space_constraint(a, pltpu.HBM)
        for a in (owner_orders.T, legendre, beam_fringe_harmonics, visibility)
    ]
    blocks, spectra = gather(*in_hbm)
    return normal_maps(blocks, spectra)


def solution(mesh):
    return jax.shard_map(
        on_device,
        mesh=mesh,
        in_specs=(P("bl", None, None, None), P(None, "ma", None), P("bl", None, "ma"), P()),
        out_specs=(P("ma", None, "bl", None), P("ma", None, "bl")),
        check_vma=False,
    )
```

```python
import functools
import math

import jax
import jax.numpy as jnp
from jax import lax
from jax.experimental import pallas as pl
from jax.experimental.pallas import tpu as pltpu
from jax.sharding import PartitionSpec as P

F32 = jnp.float32
BF16 = jnp.bfloat16
MESH = pl.DeviceIdType.MESH

NZ = 4
NY = 4
NX = 4
CAP = 4
ORDERS = 32
DEG = 96
PACK = 112
ROWS = 32
COLS = 1536
GROUP = 8


def gather_kernel(
    orders_ref, legendre_ref, beam_ref, visibility_ref,
    held, spectra,
    orders, legendre, beam, visibility, products, harmonic, outgoing, arrived,
    crossed, lined,
    legendre_sem, beam_sem, small_sem, a_send, a_recv, k_send, k_recv, l_send, l_recv, p_send, p_recv,
    x_send, x_recv, c_send, c_recv, s_send, s_recv,
):
    bl = lax.axis_index("bl")
    ma = lax.axis_index("ma")
    x, core = bl // 2, bl % 2
    z, y = ma // NY, ma % NY
    right = ((x + 1) % NX) * 2 + core
    left = ((x + NX - 1) % NX) * 2 + core
    across = ((x + 2) % NX) * 2 + core
    sibling = x * 2 + (1 - core)

    visibility_load = pltpu.make_async_copy(visibility_ref, visibility, small_sem.at[0])
    visibility_load.start()
    loads = []
    for g in range(ORDERS // GROUP):
        part = pl.ds(g * GROUP, GROUP)
        pair = (
            pltpu.make_async_copy(beam_ref.at[:, part], beam.at[:, part], beam_sem.at[g]),
            pltpu.make_async_copy(legendre_ref.at[part], legendre.at[part], legendre_sem.at[g]),
        )
        for load in pair:
            load.start()
        loads.append(pair)
    orders_load = pltpu.make_async_copy(orders_ref, orders, small_sem.at[1])
    orders_load.start()

    barrier = pltpu.get_barrier_semaphore()
    for d in range(1, NZ * NY):
        peer = ((z + d // NY) % NZ) * NY + (y + d) % NY
        pl.semaphore_signal(barrier, inc=1, device_id={"bl": bl, "ma": peer}, device_id_type=MESH)
    for d in range(1, 2 * NX):
        peer = (bl + d) % (2 * NX)
        pl.semaphore_signal(barrier, inc=1, device_id={"bl": peer, "ma": ma}, device_id_type=MESH)

    times = visibility_ref.shape[2]
    total_time = times * NZ * NY
    order_index = lax.broadcasted_iota(jnp.int32, (ORDERS, times), 0)
    time_index = lax.broadcasted_iota(jnp.int32, (ORDERS, times), 1) + ma * times
    angle = ((order_index * time_index) & (total_time - 1)).astype(F32) * (2.0 * math.pi / total_time)
    cosine, sine = jnp.cos(angle), jnp.sin(angle)
    visibility_load.wait()
    real = visibility[:, 0, :]
    imag = visibility[:, 1, :]
    direct = jnp.concatenate([real, imag] * CAP, axis=0)
    turned = jnp.concatenate([imag, -real] * CAP, axis=0)
    contract = (((1,), (1,)), ((), ()))
    partial = (
        lax.dot_general(cosine, direct, contract, precision=lax.Precision.HIGHEST, preferred_element_type=F32)
        + lax.dot_general(sine, turned, contract, precision=lax.Precision.HIGHEST, preferred_element_type=F32)
    ) * (1.0 / math.sqrt(total_time))
    high = partial.astype(BF16).astype(F32)
    low = partial - high
    row = lax.broadcasted_iota(jnp.int32, (PACK - DEG, 128), 0)
    for m in range(ORDERS):
        harmonic[m, DEG:PACK, :] = jnp.where(
            row == 0, high[m : m + 1], jnp.where(row == 1, low[m : m + 1], 0.0)
        ).astype(BF16)
    harmonic[ORDERS] = jnp.zeros((PACK, 128), BF16)

    part = GROUP // 2
    for g in range(ORDERS // GROUP):
        for load in loads[g]:
            load.wait()
        for first in range(0, GROUP, part):
            product = lax.dot_general(
                legendre[g * GROUP + first : g * GROUP + first + part].reshape(part * DEG, -1),
                beam[:, g * GROUP : (g + 1) * GROUP].reshape(GROUP * ROWS, -1),
                contract,
                preferred_element_type=F32,
            ).astype(BF16)
            for i in range(part):
                products[first + i, g * DEG : (g + 1) * DEG] = product[i * DEG : (i + 1) * DEG]
    source = lax.broadcasted_iota(jnp.int32, (GROUP * ROWS, 128), 0)
    column = lax.broadcasted_iota(jnp.int32, (GROUP * ROWS, 128), 1) % ROWS
    wanted = (column % (ROWS // 2)) * (2 * GROUP) + column // (ROWS // 2)
    for i in range(GROUP):
        pick = (source == wanted + 2 * i).astype(F32).astype(BF16)
        picked = jnp.dot(products[i], pick, preferred_element_type=F32).astype(BF16)
        for g in range(ORDERS // GROUP):
            harmonic[g * GROUP + i, 0:DEG, :] = picked[g * DEG : (g + 1) * DEG]
    orders_load.wait()

    pl.semaphore_wait(barrier, NZ * NY - 1 + 2 * NX - 1)

    def row(t, at_y):
        sign = 1 - 2 * (at_y % 2)
        return (0, sign, -sign, 2)[t]

    def owner_at(t, dy):
        at_y = (y + dy) % NY
        return (z + NZ - row(t, at_y)) % NZ, at_y

    slot_lane = lax.broadcasted_iota(jnp.int32, (PACK, 128), 1) // ROWS

    def block_for(at_z, at_y):
        owner = at_z * NY + at_y
        parts = [harmonic[orders[s, owner]] for s in range(CAP)]
        return jnp.where(
            slot_lane < 2,
            jnp.where(slot_lane == 0, parts[0], parts[1]),
            jnp.where(slot_lane == 2, parts[2], parts[3]),
        )

    def send(source, target, send_sem, recv_sem, to_bl, to_ma):
        pltpu.make_async_remote_copy(
            src_ref=source, dst_ref=target, send_sem=send_sem, recv_sem=recv_sem,
            device_id={"bl": to_bl, "ma": to_ma}, device_id_type=MESH,
        ).start()

    def await_bytes(ref, sem):
        pltpu.make_async_copy(ref, ref, sem).wait()

    for t in (1, 0):
        for dy in range(NY):
            at_z, at_y = owner_at(t, dy)
            block = block_for(at_z, at_y)
            crossed[x, t, at_y] = block[0:DEG]
            if t or dy:
                outgoing[t * NY + dy, DEG:PACK] = block[DEG:PACK]
            else:
                arrived[ma, DEG:PACK] = block[DEG:PACK]
        lower, upper = (crossed.at[x, t, pl.ds(h * (NY // 2), NY // 2)] for h in range(2))
        send(lower, lower, k_send, k_recv.at[t, 0], right, ma)
        send(upper, upper, k_send, k_recv.at[t, 1], left, ma)
        send(upper, upper, k_send, k_recv.at[t, 3], right, ma)
        send(lower, lower, k_send, k_recv.at[t, 4], left, ma)

    for t in (2, 3):
        for dy in range(NY):
            at_z, at_y = owner_at(t, dy)
            n = t * NY + dy
            outgoing[n] = block_for(at_z, at_y)
            send(outgoing.at[n], arrived.at[ma], a_send, a_recv.at[t - 2], bl, at_z * NY + at_y)

    def pass_on(t, n, who):
        for dy in range(NY):
            if t or dy:
                at_z, at_y = owner_at(t, dy)
                send(crossed.at[who // 2, t, at_y], lined.at[t, who // 2, y],
                     l_send.at[t], l_recv.at[t, n], bl, at_z * NY + at_y)

    pass_on(1, 0, bl)
    pass_on(0, 0, bl)
    for t in (1, 0):
        for dy in range(NY):
            if t or dy:
                at_z, at_y = owner_at(t, dy)
                send(outgoing.at[t * NY + dy, pl.ds(DEG, PACK - DEG)], arrived.at[ma, pl.ds(DEG, PACK - DEG)],
                     p_send, p_recv, bl, at_z * NY + at_y)

    def cross_near(t):
        half = crossed.at[left // 2, t, pl.ds(0, NY // 2)]
        await_bytes(half, k_recv.at[t, 0])
        send(half, half, k_send, k_recv.at[t, 2], right, ma)
        half = crossed.at[right // 2, t, pl.ds(NY // 2, NY // 2)]
        await_bytes(half, k_recv.at[t, 1])
        send(half, half, k_send, k_recv.at[t, 2], left, ma)
        await_bytes(half, k_recv.at[t, 3])
        pass_on(t, 1, left)
        await_bytes(half, k_recv.at[t, 4])
        pass_on(t, 2, right)

    def cross_far(t):
        await_bytes(crossed.at[across // 2, t], k_recv.at[t, 2])
        pass_on(t, 3, across)

    def view(t, who, first=0, count=CAP):
        return held.at[(z + NZ + row(t, y)) % NZ, who, pl.ds(first, count)]

    def to_sibling(t, who):
        ref = view(t, who)
        send(ref, ref, c_send, c_recv, sibling, ma)

    def keep(t, who, blocks):
        stacked = jnp.concatenate(blocks, axis=0)
        held[(z + NZ + row(t, y)) % NZ, who] = stacked.T.reshape(CAP, ROWS, NY * DEG)

    def collect(t, n, who):
        await_bytes(lined.at[t, 0, pl.ds(0, NY if t else NY - 1)], l_recv.at[t, n])
        if t == 0:
            lined[t, who // 2, y] = crossed[who // 2, t, y]
        keep(t, who, [lined[t, who // 2, j] for j in range(NY)])
        to_sibling(t, who)

    def own_part(t):
        await_bytes(arrived.at[pl.ds(0, NY)], a_recv.at[t - 2])
        at_z = (z + NZ + row(t, y)) % NZ
        keep(t, bl, [arrived[at_z * NY + j, 0:DEG, :] for j in range(NY)])
        lower, upper = (view(t, bl, h * (CAP // 2), CAP // 2) for h in range(2))
        send(lower, lower, x_send, x_recv.at[t - 2, 0], right, ma)
        send(upper, upper, x_send, x_recv.at[t - 2, 1], left, ma)
        send(upper, upper, x_send, x_recv.at[t - 2, 3], right, ma)
        send(lower, lower, x_send, x_recv.at[t - 2, 4], left, ma)
        to_sibling(t, bl)

    def near_part(t):
        half = view(t, left, 0, CAP // 2)
        await_bytes(half, x_recv.at[t - 2, 0])
        send(half, half, x_send, x_recv.at[t - 2, 2], right, ma)
        half = view(t, right, CAP // 2, CAP // 2)
        await_bytes(half, x_recv.at[t - 2, 1])
        send(half, half, x_send, x_recv.at[t - 2, 2], left, ma)
        await_bytes(half, x_recv.at[t - 2, 3])
        to_sibling(t, left)
        await_bytes(half, x_recv.at[t - 2, 4])
        to_sibling(t, right)

    def far_part(t):
        await_bytes(view(t, across), x_recv.at[t - 2, 2])
        to_sibling(t, across)

    cross_near(1)
    cross_near(0)
    own_part(2)
    own_part(3)
    cross_far(1)
    cross_far(0)
    collect(1, 0, bl)
    collect(0, 0, bl)

    await_bytes(arrived.at[pl.ds(0, 2 * NY - 1), pl.ds(DEG, PACK - DEG)], p_recv)
    total = jnp.zeros((PACK - DEG, 128), F32)
    for k in range(NZ * NY):
        total = total + arrived[k, DEG:PACK, :].astype(F32)
    line = jnp.sum(total, axis=0, keepdims=True).astype(BF16).astype(F32)
    spectra[bl] = jnp.broadcast_to(line, (8, 128))
    for d in range(1, 2 * NX):
        send(spectra.at[bl], spectra.at[bl], s_send, s_recv, (bl + d) % (2 * NX), ma)

    collect(1, 1, left)
    collect(1, 2, right)
    collect(0, 1, left)
    collect(0, 2, right)
    near_part(2)
    near_part(3)
    collect(1, 3, across)
    collect(0, 3, across)
    far_part(2)
    far_part(3)

    await_bytes(held.at[pl.ds(0, NZ // 2)], c_recv)
    await_bytes(spectra.at[pl.ds(0, 2 * NX - 1)], s_recv)
    await_bytes(crossed.at[pl.ds(0, NX - 1)], k_send)
    await_bytes(outgoing.at[pl.ds(0, 2 * NY)], a_send)
    await_bytes(outgoing.at[pl.ds(0, 2 * NY - 1), pl.ds(DEG, PACK - DEG)], p_send)
    await_bytes(crossed.at[pl.ds(0, NX - 1), 0], l_send.at[0])
    await_bytes(crossed.at[:, 1], l_send.at[1])
    await_bytes(held.at[0, pl.ds(0, NX + 2)], x_send)
    await_bytes(held.at[pl.ds(0, NZ // 2)], c_send)
    await_bytes(spectra.at[pl.ds(0, 2 * NX - 1)], s_send)


def gather(orders, legendre, beam, visibility):
    hbm = pl.BlockSpec(memory_space=pltpu.HBM)
    vmem = pl.BlockSpec(memory_space=pltpu.VMEM)
    dma = pltpu.SemaphoreType.DMA
    return pl.pallas_call(
        gather_kernel,
        out_shape=(
            jax.ShapeDtypeStruct((NZ, 2 * NX, CAP, ROWS, NY * DEG), BF16),
            jax.ShapeDtypeStruct((2 * NX, 8, 128), F32),
        ),
        in_specs=[
            hbm,
            hbm,
            hbm,
            hbm,
        ],
        out_specs=(vmem, vmem),
        scratch_shapes=[
            pltpu.SMEM(orders.shape, jnp.int32),
            pltpu.VMEM(legendre.shape, BF16),
            pltpu.VMEM(beam.shape, BF16),
            pltpu.VMEM(visibility.shape, F32),
            pltpu.VMEM((GROUP, ORDERS // GROUP * DEG, GROUP * ROWS), BF16),
            pltpu.VMEM((ORDERS + 1, PACK, 128), BF16),
            pltpu.VMEM((NZ * NY, PACK, 128), BF16),
            pltpu.VMEM((NZ * NY, PACK, 128), BF16),
            pltpu.VMEM((NX, 2, NY, DEG, 128), BF16),
            pltpu.VMEM((2, NX, NY, DEG, 128), BF16),
            dma((ORDERS // GROUP,)),
            dma((ORDERS // GROUP,)),
            dma((2,)),
            dma,
            dma((2,)),
            dma,
            dma((2, 5)),
            dma((2,)),
            dma((2, 4)),
            dma,
            dma,
            dma,
            dma((2, 5)),
            dma,
            dma,
            dma,
            dma,
        ],
        compiler_params=pltpu.CompilerParams(
            collective_id=0, has_side_effects=True, vmem_limit_bytes=40 * 1024 * 1024
        ),
        name="gather_blocks",
    )(orders, legendre, beam, visibility)


def normal_kernel(blocks_ref, spectra_ref, normal_ref, map_ref, own, turned, result, maps, out_sem):
    bl = lax.axis_index("bl")
    start = pl.multiple_of((bl % 2) * 128, 128)
    skip = pl.multiple_of((bl % 2) * 64, 16)
    scale = 1.0 / 128.0
    width = NY * DEG
    copies = []

    def prepare(s):
        window = blocks_ref[bl // 2, :, s, :, pl.ds(start, 256)].reshape(2 * NX * ROWS, 256)
        pieces = []
        for k in range(2 * NX):
            pieces.append(-window[k * ROWS + ROWS // 2 : (k + 1) * ROWS])
            pieces.append(window[k * ROWS : k * ROWS + ROWS // 2])
        own[s] = window.T
        turned[s] = jnp.concatenate(pieces, axis=0).T

    for s in range(CAP):
        prepare(s)
        left = jnp.concatenate([own[s, pl.ds(skip, 192), :], turned[s, pl.ds(skip, 192), :]], axis=0)
        for n in range(0, NZ, 2):
            right = jnp.concatenate(
                [blocks_ref[n + h, :, s].reshape(2 * NX * ROWS, width) for h in range(2)], axis=1
            )
            product = jnp.dot(left, right, preferred_element_type=F32) * scale
            part = pl.ds(n * width, 2 * width)
            result[s, 0, :, part] = product[0:192].astype(BF16)
            result[s, 1, :, part] = product[192:384].astype(BF16)
            copy = pltpu.make_async_copy(
                result.at[s, :, :, part], normal_ref.at[s, :, :, part], out_sem.at[s * (NZ // 2) + n // 2]
            )
            copy.start()
            copies.append(copy)
    lane = lax.broadcasted_iota(jnp.int32, (8, 128), 1) // ROWS
    for s in range(CAP):
        left = jnp.concatenate([own[s, pl.ds(skip, 192), :], turned[s, pl.ds(skip, 192), :]], axis=0)
        halves = []
        for h in range(2):
            line = jnp.zeros((8, 128), F32)
            for q in range(4):
                moved = pltpu.roll(spectra_ref[h * 4 + q], (q * ROWS + 128 - s * ROWS) % 128, 1)
                line = jnp.where(lane == q, moved, line)
            halves.append(line)
        spectrum = jnp.concatenate(halves, axis=1).astype(BF16)
        adjoint = lax.dot_general(spectrum, left, (((1,), (1,)), ((), ())), preferred_element_type=F32)
        adjoint = adjoint * (1.0 / math.sqrt(128.0))
        maps[s, 0:1, :] = adjoint[0:1, 0:192]
        maps[s, 1:2, :] = adjoint[0:1, 192:384]
    copy = pltpu.make_async_copy(maps, map_ref, out_sem.at[CAP * NZ // 2])
    copy.start()
    copies.append(copy)
    for copy in copies:
        copy.wait()


def normal_maps(blocks, spectra):
    hbm = pl.BlockSpec(memory_space=pltpu.HBM)
    vmem = pl.BlockSpec(memory_space=pltpu.VMEM)
    return pl.pallas_call(
        normal_kernel,
        out_shape=(
            jax.ShapeDtypeStruct((CAP, 2, 192, COLS), BF16),
            jax.ShapeDtypeStruct((CAP, 2, 192), F32),
        ),
        in_specs=[vmem, vmem],
        out_specs=(hbm, hbm),
        scratch_shapes=[
            pltpu.VMEM((CAP, 256, 256), BF16),
            pltpu.VMEM((CAP, 256, 256), BF16),
            pltpu.VMEM((CAP, 2, 192, COLS), BF16),
            pltpu.VMEM((CAP, 2, 192), F32),
            pltpu.SemaphoreType.DMA((CAP * NZ // 2 + 1,)),
        ],
        compiler_params=pltpu.CompilerParams(vmem_limit_bytes=40 * 1024 * 1024),
        name="normal_maps",
    )(blocks, spectra)


def on_device(beam_fringe_harmonics, legendre, visibility, owner_orders):
    in_hbm = [
        pltpu.with_memory_space_constraint(a, pltpu.HBM)
        for a in (owner_orders.T, legendre, beam_fringe_harmonics, visibility)
    ]
    blocks, spectra = gather(*in_hbm)
    return normal_maps(blocks, spectra)


def solution(mesh):
    return jax.shard_map(
        on_device,
        mesh=mesh,
        in_specs=(P("bl", None, None, None), P(None, "ma", None), P("bl", None, "ma"), P()),
        out_specs=(P("ma", None, "bl", None), P("ma", None, "bl")),
        check_vma=False,
    )
```

```python
import functools
import math

import jax
import jax.numpy as jnp
from jax import lax
from jax.experimental import pallas as pl
from jax.experimental.pallas import tpu as pltpu
from jax.sharding import PartitionSpec as P

F32 = jnp.float32
BF16 = jnp.bfloat16
MESH = pl.DeviceIdType.MESH

NZ = 4
NY = 4
NX = 4
CAP = 4
ORDERS = 32
DEG = 96
ROWS = 32
COLS = 1536
GROUP = 8


def gather_kernel(
    orders_ref, legendre_ref, beam_ref, visibility_ref,
    held, spectra,
    orders, legendre, beam, visibility, products, harmonic, outgoing, arrived,
    crossed, lined, series, leaving, partials,
    legendre_sem, beam_sem, small_sem, a_send, a_recv, k_send, k_recv, l_send, l_recv, p_send, p_recv,
    x_send, x_recv, c_send, c_recv, s_send, s_recv,
):
    bl = lax.axis_index("bl")
    ma = lax.axis_index("ma")
    x, core = bl // 2, bl % 2
    z, y = ma // NY, ma % NY
    right = ((x + 1) % NX) * 2 + core
    left = ((x + NX - 1) % NX) * 2 + core
    across = ((x + 2) % NX) * 2 + core
    sibling = x * 2 + (1 - core)

    barrier = pltpu.get_barrier_semaphore()
    for dz in (2, 1, 3, 0):
        for dy in (2, 1, 3, 0):
            if dz or dy:
                peer = ((z + dz) % NZ) * NY + (y + dy) % NY
                pl.semaphore_signal(barrier, inc=1, device_id={"bl": bl, "ma": peer}, device_id_type=MESH)
    for d in range(1, 2 * NX):
        peer = (bl + d) % (2 * NX)
        pl.semaphore_signal(barrier, inc=1, device_id={"bl": peer, "ma": ma}, device_id_type=MESH)

    visibility_load = pltpu.make_async_copy(visibility_ref, visibility, small_sem.at[0])
    visibility_load.start()
    loads = []
    for g in range(ORDERS // GROUP):
        part = pl.ds(g * GROUP, GROUP)
        pair = (
            pltpu.make_async_copy(beam_ref.at[:, part], beam.at[:, part], beam_sem.at[g]),
            pltpu.make_async_copy(legendre_ref.at[part], legendre.at[part], legendre_sem.at[g]),
        )
        for load in pair:
            load.start()
        loads.append(pair)
    orders_load = pltpu.make_async_copy(orders_ref, orders, small_sem.at[1])
    orders_load.start()

    times = visibility_ref.shape[2]
    total_time = times * NZ * NY
    order_index = lax.broadcasted_iota(jnp.int32, (ORDERS, times), 0)
    time_index = lax.broadcasted_iota(jnp.int32, (ORDERS, times), 1) + ma * times
    angle = ((order_index * time_index) & (total_time - 1)).astype(F32) * (2.0 * math.pi / total_time)
    cosine, sine = jnp.cos(angle), jnp.sin(angle)
    visibility_load.wait()
    real = visibility[:, 0, :]
    imag = visibility[:, 1, :]
    direct = jnp.concatenate([real, imag] * CAP, axis=0)
    turned = jnp.concatenate([imag, -real] * CAP, axis=0)
    contract = (((1,), (1,)), ((), ()))
    partial = (
        lax.dot_general(cosine, direct, contract, precision=lax.Precision.HIGHEST, preferred_element_type=F32)
        + lax.dot_general(sine, turned, contract, precision=lax.Precision.HIGHEST, preferred_element_type=F32)
    ) * (1.0 / math.sqrt(total_time))
    for m in range(ORDERS):
        series[m] = jnp.broadcast_to(partial[m : m + 1], (8, 128))
    series[ORDERS] = jnp.zeros((8, 128), F32)
    harmonic[ORDERS] = jnp.zeros((DEG, 128), BF16)

    part = GROUP // 2
    for g in range(ORDERS // GROUP):
        for load in loads[g]:
            load.wait()
        for first in range(0, GROUP, part):
            product = lax.dot_general(
                legendre[g * GROUP + first : g * GROUP + first + part].reshape(part * DEG, -1),
                beam[:, g * GROUP : (g + 1) * GROUP].reshape(GROUP * ROWS, -1),
                contract,
                preferred_element_type=F32,
            ).astype(BF16)
            for i in range(part):
                products[first + i, g * DEG : (g + 1) * DEG] = product[i * DEG : (i + 1) * DEG]
    source = lax.broadcasted_iota(jnp.int32, (GROUP * ROWS, 128), 0)
    column = lax.broadcasted_iota(jnp.int32, (GROUP * ROWS, 128), 1) % ROWS
    wanted = (column % (ROWS // 2)) * (2 * GROUP) + column // (ROWS // 2)
    for i in range(GROUP):
        pick = (source == wanted + 2 * i).astype(F32).astype(BF16)
        picked = jnp.dot(products[i], pick, preferred_element_type=F32).astype(BF16)
        for g in range(ORDERS // GROUP):
            harmonic[g * GROUP + i] = picked[g * DEG : (g + 1) * DEG]
    orders_load.wait()

    pl.semaphore_wait(barrier, NZ * NY - 1 + 2 * NX - 1)

    row = (0, 1, 2, NZ - 1)

    def owner_at(t, dy):
        return (z + NZ - row[t]) % NZ, (y + dy) % NY

    def for_owner(parts):
        slot = lax.broadcasted_iota(jnp.int32, parts[0].shape, 1) // ROWS
        return jnp.where(
            slot < 2,
            jnp.where(slot == 0, parts[0], parts[1]),
            jnp.where(slot == 2, parts[2], parts[3]),
        )

    def block_for(at_z, at_y):
        owner = at_z * NY + at_y
        return for_owner([harmonic[orders[s, owner]] for s in range(CAP)])

    def send(source, target, send_sem, recv_sem, to_bl, to_ma):
        pltpu.make_async_remote_copy(
            src_ref=source, dst_ref=target, send_sem=send_sem, recv_sem=recv_sem,
            device_id={"bl": to_bl, "ma": to_ma}, device_id_type=MESH,
        ).start()

    def await_bytes(ref, sem):
        pltpu.make_async_copy(ref, ref, sem).wait()

    for t in (1, 0):
        for dy in range(NY):
            at_z, at_y = owner_at(t, dy)
            crossed[x, t, at_y] = block_for(at_z, at_y)
        lower, upper = (crossed.at[x, t, pl.ds(h * (NY // 2), NY // 2)] for h in range(2))
        send(lower, lower, k_send, k_recv.at[t, 0], right, ma)
        send(upper, upper, k_send, k_recv.at[t, 1], left, ma)
        send(upper, upper, k_send, k_recv.at[t, 3], right, ma)
        send(lower, lower, k_send, k_recv.at[t, 4], left, ma)

    for t in (2, 3):
        for dy in (2, 1, 3, 0):
            at_z, at_y = owner_at(t, dy)
            n = (t - 2) * NY + dy
            outgoing[n] = block_for(at_z, at_y)
            send(outgoing.at[n], arrived.at[ma], a_send, a_recv.at[t - 2], bl, at_z * NY + at_y)

    def pass_on(t, n, who):
        for dy in (2, 1, 3, 0):
            if t or dy:
                at_z, at_y = owner_at(t, dy)
                send(crossed.at[who // 2, t, at_y], lined.at[t, who // 2, y],
                     l_send.at[t], l_recv.at[t, n], bl, at_z * NY + at_y)

    pass_on(1, 0, bl)
    pass_on(0, 0, bl)
    for d in range(NZ * NY):
        peer = ((z + d // NY) % NZ) * NY + (y + d) % NY
        line = for_owner([series[orders[s, peer]] for s in range(CAP)])
        if d == 0:
            partials[ma] = line
        else:
            leaving[d - 1] = line
            send(leaving.at[d - 1], partials.at[ma], p_send, p_recv, bl, peer)

    def cross_near(t):
        half = crossed.at[left // 2, t, pl.ds(0, NY // 2)]
        await_bytes(half, k_recv.at[t, 0])
        send(half, half, k_send, k_recv.at[t, 2], right, ma)
        half = crossed.at[right // 2, t, pl.ds(NY // 2, NY // 2)]
        await_bytes(half, k_recv.at[t, 1])
        send(half, half, k_send, k_recv.at[t, 2], left, ma)
        await_bytes(half, k_recv.at[t, 3])
        pass_on(t, 1, left)
        await_bytes(half, k_recv.at[t, 4])
        pass_on(t, 2, right)

    def cross_far(t):
        await_bytes(crossed.at[across // 2, t], k_recv.at[t, 2])
        pass_on(t, 3, across)

    def view(t, who, first=0, count=CAP):
        return held.at[(z + row[t]) % NZ, who, pl.ds(first, count)]

    def to_sibling(t, who):
        ref = view(t, who)
        send(ref, ref, c_send, c_recv, sibling, ma)

    def keep(t, who, blocks):
        stacked = jnp.concatenate(blocks, axis=0)
        held[(z + row[t]) % NZ, who] = stacked.T.reshape(CAP, ROWS, NY * DEG)

    def collect(t, n, who):
        await_bytes(lined.at[t, 0, pl.ds(0, NY if t else NY - 1)], l_recv.at[t, n])
        if t == 0:
            lined[t, who // 2, y] = crossed[who // 2, t, y]
        keep(t, who, [lined[t, who // 2, j] for j in range(NY)])
        to_sibling(t, who)

    def own_part(t):
        await_bytes(arrived.at[pl.ds(0, NY)], a_recv.at[t - 2])
        at_z = (z + row[t]) % NZ
        keep(t, bl, [arrived[at_z * NY + j] for j in range(NY)])
        lower, upper = (view(t, bl, h * (CAP // 2), CAP // 2) for h in range(2))
        send(lower, lower, x_send, x_recv.at[t - 2, 0], right, ma)
        send(upper, upper, x_send, x_recv.at[t - 2, 1], left, ma)
        send(upper, upper, x_send, x_recv.at[t - 2, 3], right, ma)
        send(lower, lower, x_send, x_recv.at[t - 2, 4], left, ma)
        to_sibling(t, bl)

    def near_part(t):
        half = view(t, left, 0, CAP // 2)
        await_bytes(half, x_recv.at[t - 2, 0])
        send(half, half, x_send, x_recv.at[t - 2, 2], right, ma)
        half = view(t, right, CAP // 2, CAP // 2)
        await_bytes(half, x_recv.at[t - 2, 1])
        send(half, half, x_send, x_recv.at[t - 2, 2], left, ma)
        await_bytes(half, x_recv.at[t - 2, 3])
        to_sibling(t, left)
        await_bytes(half, x_recv.at[t - 2, 4])
        to_sibling(t, right)

    def far_part(t):
        await_bytes(view(t, across), x_recv.at[t - 2, 2])
        to_sibling(t, across)

    cross_near(1)
    cross_near(0)
    own_part(2)
    own_part(3)
    cross_far(1)
    cross_far(0)
    collect(1, 0, bl)
    collect(0, 0, bl)
    near_part(2)
    collect(1, 1, left)
    collect(1, 2, right)
    near_part(3)
    collect(0, 1, left)
    collect(0, 2, right)
    await_bytes(leaving, p_recv)
    line = jnp.sum(partials[...], axis=0)[0:1].astype(BF16).astype(F32)
    spectra[bl] = jnp.broadcast_to(line, (8, 128))
    for d in range(1, 2 * NX):
        send(spectra.at[bl], spectra.at[bl], s_send, s_recv, (bl + d) % (2 * NX), ma)

    collect(1, 3, across)
    far_part(2)
    collect(0, 3, across)
    far_part(3)

    await_bytes(held.at[pl.ds(0, NZ // 2)], c_recv)
    await_bytes(spectra.at[pl.ds(0, 2 * NX - 1)], s_recv)
    await_bytes(crossed.at[pl.ds(0, NX - 1)], k_send)
    await_bytes(outgoing, a_send)
    await_bytes(leaving, p_send)
    await_bytes(crossed.at[pl.ds(0, NX - 1), 0], l_send.at[0])
    await_bytes(crossed.at[:, 1], l_send.at[1])
    await_bytes(held.at[0, pl.ds(0, NX + 2)], x_send)
    await_bytes(held.at[pl.ds(0, NZ // 2)], c_send)
    await_bytes(spectra.at[pl.ds(0, 2 * NX - 1)], s_send)


def gather(orders, legendre, beam, visibility):
    hbm = pl.BlockSpec(memory_space=pltpu.HBM)
    vmem = pl.BlockSpec(memory_space=pltpu.VMEM)
    dma = pltpu.SemaphoreType.DMA
    return pl.pallas_call(
        gather_kernel,
        out_shape=(
            jax.ShapeDtypeStruct((NZ, 2 * NX, CAP, ROWS, NY * DEG), BF16),
            jax.ShapeDtypeStruct((2 * NX, 8, 128), F32),
        ),
        in_specs=[
            hbm,
            hbm,
            hbm,
            hbm,
        ],
        out_specs=(vmem, vmem),
        scratch_shapes=[
            pltpu.SMEM(orders.shape, jnp.int32),
            pltpu.VMEM(legendre.shape, BF16),
            pltpu.VMEM(beam.shape, BF16),
            pltpu.VMEM(visibility.shape, F32),
            pltpu.VMEM((GROUP, ORDERS // GROUP * DEG, GROUP * ROWS), BF16),
            pltpu.VMEM((ORDERS + 1, DEG, 128), BF16),
            pltpu.VMEM((2 * NY, DEG, 128), BF16),
            pltpu.VMEM((NZ * NY, DEG, 128), BF16),
            pltpu.VMEM((NX, 2, NY, DEG, 128), BF16),
            pltpu.VMEM((2, NX, NY, DEG, 128), BF16),
            pltpu.VMEM((ORDERS + 1, 8, 128), F32),
            pltpu.VMEM((NZ * NY - 1, 8, 128), F32),
            pltpu.VMEM((NZ * NY, 8, 128), F32),
            dma((ORDERS // GROUP,)),
            dma((ORDERS // GROUP,)),
            dma((2,)),
            dma,
            dma((2,)),
            dma,
            dma((2, 5)),
            dma((2,)),
            dma((2, 4)),
            dma,
            dma,
            dma,
            dma((2, 5)),
            dma,
            dma,
            dma,
            dma,
        ],
        compiler_params=pltpu.CompilerParams(
            collective_id=0, has_side_effects=True, vmem_limit_bytes=40 * 1024 * 1024
        ),
        name="gather_blocks",
    )(orders, legendre, beam, visibility)


def normal_kernel(blocks_ref, spectra_ref, normal_ref, map_ref, own, turned, result, maps, out_sem):
    bl = lax.axis_index("bl")
    start = pl.multiple_of((bl % 2) * 128, 128)
    skip = pl.multiple_of((bl % 2) * 64, 16)
    scale = 1.0 / 128.0
    width = NY * DEG
    copies = []

    def prepare(s):
        window = blocks_ref[bl // 2, :, s, :, pl.ds(start, 256)].reshape(2 * NX * ROWS, 256)
        pieces = []
        for k in range(2 * NX):
            pieces.append(-window[k * ROWS + ROWS // 2 : (k + 1) * ROWS])
            pieces.append(window[k * ROWS : k * ROWS + ROWS // 2])
        own[s] = window.T
        turned[s] = jnp.concatenate(pieces, axis=0).T

    for s in range(CAP):
        prepare(s)
        left = jnp.concatenate([own[s, pl.ds(skip, 192), :], turned[s, pl.ds(skip, 192), :]], axis=0)
        for n in range(0, NZ, 2):
            right = jnp.concatenate(
                [blocks_ref[n + h, :, s].reshape(2 * NX * ROWS, width) for h in range(2)], axis=1
            )
            product = jnp.dot(left, right, preferred_element_type=F32) * scale
            part = pl.ds(n * width, 2 * width)
            result[s, 0, :, part] = product[0:192].astype(BF16)
            result[s, 1, :, part] = product[192:384].astype(BF16)
            copy = pltpu.make_async_copy(
                result.at[s, :, :, part], normal_ref.at[s, :, :, part], out_sem.at[s * (NZ // 2) + n // 2]
            )
            copy.start()
            copies.append(copy)
    lane = lax.broadcasted_iota(jnp.int32, (8, 128), 1) // ROWS
    for s in range(CAP):
        left = jnp.concatenate([own[s, pl.ds(skip, 192), :], turned[s, pl.ds(skip, 192), :]], axis=0)
        halves = []
        for h in range(2):
            line = jnp.zeros((8, 128), F32)
            for q in range(4):
                moved = pltpu.roll(spectra_ref[h * 4 + q], (q * ROWS + 128 - s * ROWS) % 128, 1)
                line = jnp.where(lane == q, moved, line)
            halves.append(line)
        spectrum = jnp.concatenate(halves, axis=1).astype(BF16)
        adjoint = lax.dot_general(spectrum, left, (((1,), (1,)), ((), ())), preferred_element_type=F32)
        adjoint = adjoint * (1.0 / math.sqrt(128.0))
        maps[s, 0:1, :] = adjoint[0:1, 0:192]
        maps[s, 1:2, :] = adjoint[0:1, 192:384]
    copy = pltpu.make_async_copy(maps, map_ref, out_sem.at[CAP * NZ // 2])
    copy.start()
    copies.append(copy)
    for copy in copies:
        copy.wait()


def normal_maps(blocks, spectra):
    hbm = pl.BlockSpec(memory_space=pltpu.HBM)
    vmem = pl.BlockSpec(memory_space=pltpu.VMEM)
    return pl.pallas_call(
        normal_kernel,
        out_shape=(
            jax.ShapeDtypeStruct((CAP, 2, 192, COLS), BF16),
            jax.ShapeDtypeStruct((CAP, 2, 192), F32),
        ),
        in_specs=[vmem, vmem],
        out_specs=(hbm, hbm),
        scratch_shapes=[
            pltpu.VMEM((CAP, 256, 256), BF16),
            pltpu.VMEM((CAP, 256, 256), BF16),
            pltpu.VMEM((CAP, 2, 192, COLS), BF16),
            pltpu.VMEM((CAP, 2, 192), F32),
            pltpu.SemaphoreType.DMA((CAP * NZ // 2 + 1,)),
        ],
        compiler_params=pltpu.CompilerParams(vmem_limit_bytes=40 * 1024 * 1024),
        name="normal_maps",
    )(blocks, spectra)


def on_device(beam_fringe_harmonics, legendre, visibility, owner_orders):
    in_hbm = [
        pltpu.with_memory_space_constraint(a, pltpu.HBM)
        for a in (owner_orders.T, legendre, beam_fringe_harmonics, visibility)
    ]
    blocks, spectra = gather(*in_hbm)
    return normal_maps(blocks, spectra)


def solution(mesh):
    return jax.shard_map(
        on_device,
        mesh=mesh,
        in_specs=(P("bl", None, None, None), P(None, "ma", None), P("bl", None, "ma"), P()),
        out_specs=(P("ma", None, "bl", None), P("ma", None, "bl")),
        check_vma=False,
    )
```

```python
import functools
import math

import jax
import jax.numpy as jnp
from jax import lax
from jax.experimental import pallas as pl
from jax.experimental.pallas import tpu as pltpu
from jax.sharding import PartitionSpec as P

F32 = jnp.float32
BF16 = jnp.bfloat16
MESH = pl.DeviceIdType.MESH

NZ = 4
NY = 4
NX = 4
CAP = 4
ORDERS = 32
DEG = 96
ROWS = 32
COLS = 1536
GROUP = 8


def gather_kernel(
    orders_ref, legendre_ref, beam_ref, visibility_ref,
    held, spectra,
    orders, legendre, beam, visibility, products, harmonic, outgoing, arrived,
    crossed, lined, series, leaving, partials,
    legendre_sem, beam_sem, small_sem, a_send, a_recv, k_send, k_recv, l_send, l_recv, p_send, p_recv,
    x_send, x_recv, c_send, c_recv, s_send, s_recv,
):
    bl = lax.axis_index("bl")
    ma = lax.axis_index("ma")
    x, core = bl // 2, bl % 2
    z, y = ma // NY, ma % NY
    right = ((x + 1) % NX) * 2 + core
    left = ((x + NX - 1) % NX) * 2 + core
    across = ((x + 2) % NX) * 2 + core
    sibling = x * 2 + (1 - core)

    barrier = pltpu.get_barrier_semaphore()
    for dz in (2, 1, 3, 0):
        for dy in (2, 1, 3, 0):
            if dz or dy:
                peer = ((z + dz) % NZ) * NY + (y + dy) % NY
                pl.semaphore_signal(barrier, inc=1, device_id={"bl": bl, "ma": peer}, device_id_type=MESH)
    for d in range(1, 2 * NX):
        peer = (bl + d) % (2 * NX)
        pl.semaphore_signal(barrier, inc=1, device_id={"bl": peer, "ma": ma}, device_id_type=MESH)

    visibility_load = pltpu.make_async_copy(visibility_ref, visibility, small_sem.at[0])
    visibility_load.start()
    loads = []
    for g in range(ORDERS // GROUP):
        part = pl.ds(g * GROUP, GROUP)
        pair = (
            pltpu.make_async_copy(beam_ref.at[:, part], beam.at[:, part], beam_sem.at[g]),
            pltpu.make_async_copy(legendre_ref.at[part], legendre.at[part], legendre_sem.at[g]),
        )
        for load in pair:
            load.start()
        loads.append(pair)
    orders_load = pltpu.make_async_copy(orders_ref, orders, small_sem.at[1])
    orders_load.start()

    times = visibility_ref.shape[2]
    total_time = times * NZ * NY
    order_index = lax.broadcasted_iota(jnp.int32, (ORDERS, times), 0)
    time_index = lax.broadcasted_iota(jnp.int32, (ORDERS, times), 1) + ma * times
    angle = ((order_index * time_index) & (total_time - 1)).astype(F32) * (2.0 * math.pi / total_time)
    cosine, sine = jnp.cos(angle), jnp.sin(angle)
    visibility_load.wait()
    real = visibility[:, 0, :]
    imag = visibility[:, 1, :]
    direct = jnp.concatenate([real, imag] * CAP, axis=0)
    turned = jnp.concatenate([imag, -real] * CAP, axis=0)
    contract = (((1,), (1,)), ((), ()))
    partial = (
        lax.dot_general(cosine, direct, contract, precision=lax.Precision.HIGHEST, preferred_element_type=F32)
        + lax.dot_general(sine, turned, contract, precision=lax.Precision.HIGHEST, preferred_element_type=F32)
    ) * (1.0 / math.sqrt(total_time))
    for m in range(ORDERS):
        series[m] = jnp.broadcast_to(partial[m : m + 1], (8, 128))
    series[ORDERS] = jnp.zeros((8, 128), F32)
    harmonic[ORDERS] = jnp.zeros((DEG, 128), BF16)

    part = GROUP // 2
    for g in range(ORDERS // GROUP):
        for load in loads[g]:
            load.wait()
        for first in range(0, GROUP, part):
            product = lax.dot_general(
                legendre[g * GROUP + first : g * GROUP + first + part].reshape(part * DEG, -1),
                beam[:, g * GROUP : (g + 1) * GROUP].reshape(GROUP * ROWS, -1),
                contract,
                preferred_element_type=F32,
            ).astype(BF16)
            for i in range(part):
                products[first + i, g * DEG : (g + 1) * DEG] = product[i * DEG : (i + 1) * DEG]
    source = lax.broadcasted_iota(jnp.int32, (GROUP * ROWS, 128), 0)
    column = lax.broadcasted_iota(jnp.int32, (GROUP * ROWS, 128), 1) % ROWS
    wanted = (column % (ROWS // 2)) * (2 * GROUP) + column // (ROWS // 2)
    for i in range(GROUP):
        pick = (source == wanted + 2 * i).astype(F32).astype(BF16)
        picked = jnp.dot(products[i], pick, preferred_element_type=F32).astype(BF16)
        for g in range(ORDERS // GROUP):
            harmonic[g * GROUP + i] = picked[g * DEG : (g + 1) * DEG]
    orders_load.wait()

    pl.semaphore_wait(barrier, NZ * NY - 1 + 2 * NX - 1)

    row = (0, 1, 2, NZ - 1)

    def owner_at(t, dy):
        return (z + NZ - row[t]) % NZ, (y + dy) % NY

    def for_owner(parts):
        slot = lax.broadcasted_iota(jnp.int32, parts[0].shape, 1) // ROWS
        return jnp.where(
            slot < 2,
            jnp.where(slot == 0, parts[0], parts[1]),
            jnp.where(slot == 2, parts[2], parts[3]),
        )

    def block_for(at_z, at_y):
        owner = at_z * NY + at_y
        return for_owner([harmonic[orders[s, owner]] for s in range(CAP)])

    def send(source, target, send_sem, recv_sem, to_bl, to_ma):
        pltpu.make_async_remote_copy(
            src_ref=source, dst_ref=target, send_sem=send_sem, recv_sem=recv_sem,
            device_id={"bl": to_bl, "ma": to_ma}, device_id_type=MESH,
        ).start()

    def await_bytes(ref, sem):
        pltpu.make_async_copy(ref, ref, sem).wait()

    for t in (1, 0):
        for dy in range(NY):
            at_z, at_y = owner_at(t, dy)
            crossed[x, t, at_y] = block_for(at_z, at_y)
        lower, upper = (crossed.at[x, t, pl.ds(h * (NY // 2), NY // 2)] for h in range(2))
        send(lower, lower, k_send, k_recv.at[t, 0], right, ma)
        send(upper, upper, k_send, k_recv.at[t, 1], left, ma)
        send(upper, upper, k_send, k_recv.at[t, 3], right, ma)
        send(lower, lower, k_send, k_recv.at[t, 4], left, ma)

    for t in (2, 3):
        for dy in (2, 1, 3, 0):
            at_z, at_y = owner_at(t, dy)
            n = (t - 2) * NY + dy
            outgoing[n] = block_for(at_z, at_y)
            send(outgoing.at[n], arrived.at[ma], a_send, a_recv.at[t - 2], bl, at_z * NY + at_y)

    def pass_on(t, n, who):
        for dy in (2, 1, 3, 0):
            if t or dy:
                at_z, at_y = owner_at(t, dy)
                send(crossed.at[who // 2, t, at_y], lined.at[t, who // 2, y],
                     l_send.at[t], l_recv.at[t, n], bl, at_z * NY + at_y)

    pass_on(1, 0, bl)
    pass_on(0, 0, bl)
    for d in range(NZ * NY):
        peer = ((z + d // NY) % NZ) * NY + (y + d) % NY
        line = for_owner([series[orders[s, peer]] for s in range(CAP)])
        if d == 0:
            partials[ma] = line
        else:
            leaving[d - 1] = line
            send(leaving.at[d - 1], partials.at[ma], p_send, p_recv, bl, peer)

    def cross_near(t):
        half = crossed.at[left // 2, t, pl.ds(0, NY // 2)]
        await_bytes(half, k_recv.at[t, 0])
        send(half, half, k_send, k_recv.at[t, 2], right, ma)
        half = crossed.at[right // 2, t, pl.ds(NY // 2, NY // 2)]
        await_bytes(half, k_recv.at[t, 1])
        send(half, half, k_send, k_recv.at[t, 2], left, ma)
        await_bytes(half, k_recv.at[t, 3])
        pass_on(t, 1, left)
        await_bytes(half, k_recv.at[t, 4])
        pass_on(t, 2, right)

    def cross_far(t):
        await_bytes(crossed.at[across // 2, t], k_recv.at[t, 2])
        pass_on(t, 3, across)

    def view(t, who, first=0, count=CAP):
        return held.at[(z + row[t]) % NZ, who, pl.ds(first, count)]

    def to_sibling(t, who):
        ref = view(t, who)
        send(ref, ref, c_send, c_recv, sibling, ma)

    def keep(t, who, blocks):
        stacked = jnp.concatenate(blocks, axis=0)
        held[(z + row[t]) % NZ, who] = stacked.T.reshape(CAP, ROWS, NY * DEG)

    def collect(t, n, who):
        await_bytes(lined.at[t, 0, pl.ds(0, NY if t else NY - 1)], l_recv.at[t, n])
        if t == 0:
            lined[t, who // 2, y] = crossed[who // 2, t, y]
        keep(t, who, [lined[t, who // 2, j] for j in range(NY)])
        to_sibling(t, who)

    def own_part(t):
        await_bytes(arrived.at[pl.ds(0, NY)], a_recv.at[t - 2])
        at_z = (z + row[t]) % NZ
        keep(t, bl, [arrived[at_z * NY + j] for j in range(NY)])
        lower, upper = (view(t, bl, h * (CAP // 2), CAP // 2) for h in range(2))
        for step in range(CAP // 2):
            ref = view(t, bl, step, 1)
            send(ref, ref, x_send, x_recv.at[t - 2, 2 * step], right, ma)
            ref = view(t, bl, CAP - 1 - step, 1)
            send(ref, ref, x_send, x_recv.at[t - 2, 2 * step + 1], left, ma)
        send(upper, upper, x_send, x_recv.at[t - 2, 5], right, ma)
        send(lower, lower, x_send, x_recv.at[t - 2, 6], left, ma)
        to_sibling(t, bl)

    def near_part(t):
        for step in range(CAP // 2):
            ref = view(t, left, step, 1)
            await_bytes(ref, x_recv.at[t - 2, 2 * step])
            send(ref, ref, x_send, x_recv.at[t - 2, 4], right, ma)
            ref = view(t, right, CAP - 1 - step, 1)
            await_bytes(ref, x_recv.at[t - 2, 2 * step + 1])
            send(ref, ref, x_send, x_recv.at[t - 2, 4], left, ma)
        half = view(t, left, 0, CAP // 2)
        await_bytes(half, x_recv.at[t - 2, 5])
        to_sibling(t, left)
        await_bytes(half, x_recv.at[t - 2, 6])
        to_sibling(t, right)

    def far_part(t):
        await_bytes(view(t, across), x_recv.at[t - 2, 4])
        to_sibling(t, across)

    cross_near(1)
    cross_near(0)
    own_part(2)
    own_part(3)
    cross_far(1)
    cross_far(0)
    collect(1, 0, bl)
    collect(0, 0, bl)
    near_part(2)
    collect(1, 1, left)
    collect(1, 2, right)
    near_part(3)
    collect(0, 1, left)
    collect(0, 2, right)
    await_bytes(leaving, p_recv)
    line = jnp.sum(partials[...], axis=0)[0:1].astype(BF16).astype(F32)
    spectra[bl] = jnp.broadcast_to(line, (8, 128))
    for d in range(1, 2 * NX):
        send(spectra.at[bl], spectra.at[bl], s_send, s_recv, (bl + d) % (2 * NX), ma)

    collect(1, 3, across)
    far_part(2)
    collect(0, 3, across)
    far_part(3)

    await_bytes(held.at[pl.ds(0, NZ // 2)], c_recv)
    await_bytes(spectra.at[pl.ds(0, 2 * NX - 1)], s_recv)
    await_bytes(crossed.at[pl.ds(0, NX - 1)], k_send)
    await_bytes(outgoing, a_send)
    await_bytes(leaving, p_send)
    await_bytes(crossed.at[pl.ds(0, NX - 1), 0], l_send.at[0])
    await_bytes(crossed.at[:, 1], l_send.at[1])
    await_bytes(held.at[0, pl.ds(0, NX + 2)], x_send)
    await_bytes(held.at[pl.ds(0, NZ // 2)], c_send)
    await_bytes(spectra.at[pl.ds(0, 2 * NX - 1)], s_send)


def gather(orders, legendre, beam, visibility):
    hbm = pl.BlockSpec(memory_space=pltpu.HBM)
    vmem = pl.BlockSpec(memory_space=pltpu.VMEM)
    dma = pltpu.SemaphoreType.DMA
    return pl.pallas_call(
        gather_kernel,
        out_shape=(
            jax.ShapeDtypeStruct((NZ, 2 * NX, CAP, ROWS, NY * DEG), BF16),
            jax.ShapeDtypeStruct((2 * NX, 8, 128), F32),
        ),
        in_specs=[
            hbm,
            hbm,
            hbm,
            hbm,
        ],
        out_specs=(vmem, vmem),
        scratch_shapes=[
            pltpu.SMEM(orders.shape, jnp.int32),
            pltpu.VMEM(legendre.shape, BF16),
            pltpu.VMEM(beam.shape, BF16),
            pltpu.VMEM(visibility.shape, F32),
            pltpu.VMEM((GROUP, ORDERS // GROUP * DEG, GROUP * ROWS), BF16),
            pltpu.VMEM((ORDERS + 1, DEG, 128), BF16),
            pltpu.VMEM((2 * NY, DEG, 128), BF16),
            pltpu.VMEM((NZ * NY, DEG, 128), BF16),
            pltpu.VMEM((NX, 2, NY, DEG, 128), BF16),
            pltpu.VMEM((2, NX, NY, DEG, 128), BF16),
            pltpu.VMEM((ORDERS + 1, 8, 128), F32),
            pltpu.VMEM((NZ * NY - 1, 8, 128), F32),
            pltpu.VMEM((NZ * NY, 8, 128), F32),
            dma((ORDERS // GROUP,)),
            dma((ORDERS // GROUP,)),
            dma((2,)),
            dma,
            dma((2,)),
            dma,
            dma((2, 5)),
            dma((2,)),
            dma((2, 4)),
            dma,
            dma,
            dma,
            dma((2, 7)),
            dma,
            dma,
            dma,
            dma,
        ],
        compiler_params=pltpu.CompilerParams(
            collective_id=0, has_side_effects=True, vmem_limit_bytes=40 * 1024 * 1024
        ),
        name="gather_blocks",
    )(orders, legendre, beam, visibility)


def normal_kernel(blocks_ref, spectra_ref, normal_ref, map_ref, own, turned, result, maps, out_sem):
    bl = lax.axis_index("bl")
    start = pl.multiple_of((bl % 2) * 128, 128)
    skip = pl.multiple_of((bl % 2) * 64, 16)
    scale = 1.0 / 128.0
    width = NY * DEG
    copies = []

    def prepare(s):
        window = blocks_ref[bl // 2, :, s, :, pl.ds(start, 256)].reshape(2 * NX * ROWS, 256)
        pieces = []
        for k in range(2 * NX):
            pieces.append(-window[k * ROWS + ROWS // 2 : (k + 1) * ROWS])
            pieces.append(window[k * ROWS : k * ROWS + ROWS // 2])
        own[s] = window.T
        turned[s] = jnp.concatenate(pieces, axis=0).T

    for s in range(CAP):
        prepare(s)
        left = jnp.concatenate([own[s, pl.ds(skip, 192), :], turned[s, pl.ds(skip, 192), :]], axis=0)
        for n in range(0, NZ, 2):
            right = jnp.concatenate(
                [blocks_ref[n + h, :, s].reshape(2 * NX * ROWS, width) for h in range(2)], axis=1
            )
            product = jnp.dot(left, right, preferred_element_type=F32) * scale
            part = pl.ds(n * width, 2 * width)
            result[s, 0, :, part] = product[0:192].astype(BF16)
            result[s, 1, :, part] = product[192:384].astype(BF16)
            copy = pltpu.make_async_copy(
                result.at[s, :, :, part], normal_ref.at[s, :, :, part], out_sem.at[s * (NZ // 2) + n // 2]
            )
            copy.start()
            copies.append(copy)
    lane = lax.broadcasted_iota(jnp.int32, (8, 128), 1) // ROWS
    for s in range(CAP):
        left = jnp.concatenate([own[s, pl.ds(skip, 192), :], turned[s, pl.ds(skip, 192), :]], axis=0)
        halves = []
        for h in range(2):
            line = jnp.zeros((8, 128), F32)
            for q in range(4):
                moved = pltpu.roll(spectra_ref[h * 4 + q], (q * ROWS + 128 - s * ROWS) % 128, 1)
                line = jnp.where(lane == q, moved, line)
            halves.append(line)
        spectrum = jnp.concatenate(halves, axis=1).astype(BF16)
        adjoint = lax.dot_general(spectrum, left, (((1,), (1,)), ((), ())), preferred_element_type=F32)
        adjoint = adjoint * (1.0 / math.sqrt(128.0))
        maps[s, 0:1, :] = adjoint[0:1, 0:192]
        maps[s, 1:2, :] = adjoint[0:1, 192:384]
    copy = pltpu.make_async_copy(maps, map_ref, out_sem.at[CAP * NZ // 2])
    copy.start()
    copies.append(copy)
    for copy in copies:
        copy.wait()


def normal_maps(blocks, spectra):
    hbm = pl.BlockSpec(memory_space=pltpu.HBM)
    vmem = pl.BlockSpec(memory_space=pltpu.VMEM)
    return pl.pallas_call(
        normal_kernel,
        out_shape=(
            jax.ShapeDtypeStruct((CAP, 2, 192, COLS), BF16),
            jax.ShapeDtypeStruct((CAP, 2, 192), F32),
        ),
        in_specs=[vmem, vmem],
        out_specs=(hbm, hbm),
        scratch_shapes=[
            pltpu.VMEM((CAP, 256, 256), BF16),
            pltpu.VMEM((CAP, 256, 256), BF16),
            pltpu.VMEM((CAP, 2, 192, COLS), BF16),
            pltpu.VMEM((CAP, 2, 192), F32),
            pltpu.SemaphoreType.DMA((CAP * NZ // 2 + 1,)),
        ],
        compiler_params=pltpu.CompilerParams(vmem_limit_bytes=40 * 1024 * 1024),
        name="normal_maps",
    )(blocks, spectra)


def on_device(beam_fringe_harmonics, legendre, visibility, owner_orders):
    in_hbm = [
        pltpu.with_memory_space_constraint(a, pltpu.HBM)
        for a in (owner_orders.T, legendre, beam_fringe_harmonics, visibility)
    ]
    blocks, spectra = gather(*in_hbm)
    return normal_maps(blocks, spectra)


def solution(mesh):
    return jax.shard_map(
        on_device,
        mesh=mesh,
        in_specs=(P("bl", None, None, None), P(None, "ma", None), P("bl", None, "ma"), P()),
        out_specs=(P("ma", None, "bl", None), P("ma", None, "bl")),
        check_vma=False,
    )
```

```python
import functools
import math

import jax
import jax.numpy as jnp
from jax import lax
from jax.experimental import pallas as pl
from jax.experimental.pallas import tpu as pltpu
from jax.sharding import PartitionSpec as P

F32 = jnp.float32
BF16 = jnp.bfloat16
MESH = pl.DeviceIdType.MESH

NZ = 4
NY = 4
NX = 4
CAP = 4
ORDERS = 32
DEG = 96
ROWS = 32
COLS = 1536
GROUP = 8


def gather_kernel(
    orders_ref, legendre_ref, beam_ref, visibility_ref,
    held, spectra,
    orders, legendre, beam, visibility, products, harmonic, outgoing, arrived,
    crossed, lined, series, leaving, partials,
    legendre_sem, beam_sem, small_sem, a_send, a_recv, k_send, k_recv, l_send, l_recv, p_send, p_recv,
    x_send, x_recv, c_send, c_recv, s_send, s_recv,
):
    bl = lax.axis_index("bl")
    ma = lax.axis_index("ma")
    x, core = bl // 2, bl % 2
    z, y = ma // NY, ma % NY
    right = ((x + 1) % NX) * 2 + core
    left = ((x + NX - 1) % NX) * 2 + core
    across = ((x + 2) % NX) * 2 + core
    sibling = x * 2 + (1 - core)

    barrier = pltpu.get_barrier_semaphore()
    for dz in (2, 1, 3, 0):
        for dy in (2, 1, 3, 0):
            if dz or dy:
                peer = ((z + dz) % NZ) * NY + (y + dy) % NY
                pl.semaphore_signal(barrier, inc=1, device_id={"bl": bl, "ma": peer}, device_id_type=MESH)
    for d in range(1, 2 * NX):
        peer = (bl + d) % (2 * NX)
        pl.semaphore_signal(barrier, inc=1, device_id={"bl": peer, "ma": ma}, device_id_type=MESH)

    visibility_load = pltpu.make_async_copy(visibility_ref, visibility, small_sem.at[0])
    visibility_load.start()
    loads = []
    for g in range(ORDERS // GROUP):
        part = pl.ds(g * GROUP, GROUP)
        pair = (
            pltpu.make_async_copy(beam_ref.at[:, part], beam.at[:, part], beam_sem.at[g]),
            pltpu.make_async_copy(legendre_ref.at[part], legendre.at[part], legendre_sem.at[g]),
        )
        for load in pair:
            load.start()
        loads.append(pair)
    orders_load = pltpu.make_async_copy(orders_ref, orders, small_sem.at[1])
    orders_load.start()

    times = visibility_ref.shape[2]
    total_time = times * NZ * NY
    order_index = lax.broadcasted_iota(jnp.int32, (ORDERS, times), 0)
    time_index = lax.broadcasted_iota(jnp.int32, (ORDERS, times), 1) + ma * times
    angle = ((order_index * time_index) & (total_time - 1)).astype(F32) * (2.0 * math.pi / total_time)
    cosine, sine = jnp.cos(angle), jnp.sin(angle)
    visibility_load.wait()
    real = visibility[:, 0, :]
    imag = visibility[:, 1, :]
    direct = jnp.concatenate([real, imag] * CAP, axis=0)
    turned = jnp.concatenate([imag, -real] * CAP, axis=0)
    contract = (((1,), (1,)), ((), ()))
    partial = (
        lax.dot_general(cosine, direct, contract, precision=lax.Precision.HIGHEST, preferred_element_type=F32)
        + lax.dot_general(sine, turned, contract, precision=lax.Precision.HIGHEST, preferred_element_type=F32)
    ) * (1.0 / math.sqrt(total_time))
    for m in range(ORDERS):
        series[m] = jnp.broadcast_to(partial[m : m + 1], (8, 128))
    series[ORDERS] = jnp.zeros((8, 128), F32)
    harmonic[ORDERS] = jnp.zeros((DEG, 128), BF16)

    part = GROUP // 2
    for g in range(ORDERS // GROUP):
        for load in loads[g]:
            load.wait()
        for first in range(0, GROUP, part):
            product = lax.dot_general(
                legendre[g * GROUP + first : g * GROUP + first + part].reshape(part * DEG, -1),
                beam[:, g * GROUP : (g + 1) * GROUP].reshape(GROUP * ROWS, -1),
                contract,
                preferred_element_type=F32,
            ).astype(BF16)
            for i in range(part):
                products[first + i, g * DEG : (g + 1) * DEG] = product[i * DEG : (i + 1) * DEG]
    source = lax.broadcasted_iota(jnp.int32, (GROUP * ROWS, 128), 0)
    column = lax.broadcasted_iota(jnp.int32, (GROUP * ROWS, 128), 1) % ROWS
    wanted = (column % (ROWS // 2)) * (2 * GROUP) + column // (ROWS // 2)
    for i in range(GROUP):
        pick = (source == wanted + 2 * i).astype(F32).astype(BF16)
        picked = jnp.dot(products[i], pick, preferred_element_type=F32).astype(BF16)
        for g in range(ORDERS // GROUP):
            harmonic[g * GROUP + i] = picked[g * DEG : (g + 1) * DEG]
    orders_load.wait()

    pl.semaphore_wait(barrier, NZ * NY - 1 + 2 * NX - 1)

    row = (0, 1, 2, NZ - 1)

    def owner_at(t, dy):
        return (z + NZ - row[t]) % NZ, (y + dy) % NY

    def for_owner(parts):
        slot = lax.broadcasted_iota(jnp.int32, parts[0].shape, 1) // ROWS
        return jnp.where(
            slot < 2,
            jnp.where(slot == 0, parts[0], parts[1]),
            jnp.where(slot == 2, parts[2], parts[3]),
        )

    def block_for(at_z, at_y):
        owner = at_z * NY + at_y
        return for_owner([harmonic[orders[s, owner]] for s in range(CAP)])

    def send(source, target, send_sem, recv_sem, to_bl, to_ma):
        pltpu.make_async_remote_copy(
            src_ref=source, dst_ref=target, send_sem=send_sem, recv_sem=recv_sem,
            device_id={"bl": to_bl, "ma": to_ma}, device_id_type=MESH,
        ).start()

    def await_bytes(ref, sem):
        pltpu.make_async_copy(ref, ref, sem).wait()

    for t in (1, 0):
        for dy in range(NY):
            at_z, at_y = owner_at(t, dy)
            crossed[x, t, at_y] = block_for(at_z, at_y)
        lower, upper = (crossed.at[x, t, pl.ds(h * (NY // 2), NY // 2)] for h in range(2))
        send(lower, lower, k_send, k_recv.at[t, 0], right, ma)
        send(upper, upper, k_send, k_recv.at[t, 1], left, ma)
        send(upper, upper, k_send, k_recv.at[t, 3], right, ma)
        send(lower, lower, k_send, k_recv.at[t, 4], left, ma)

    for t in (2, 3):
        for dy in (2, 1, 3, 0):
            at_z, at_y = owner_at(t, dy)
            n = (t - 2) * NY + dy
            outgoing[n] = block_for(at_z, at_y)
            send(outgoing.at[n], arrived.at[ma], a_send, a_recv.at[t - 2], bl, at_z * NY + at_y)

    def pass_on(t, n, who):
        for dy in (0, 1, 2, 3):
            if t or dy:
                at_z, at_y = owner_at(t, dy)
                send(crossed.at[who // 2, t, at_y], lined.at[t, who // 2, y],
                     l_send.at[t], l_recv.at[t, n], bl, at_z * NY + at_y)

    pass_on(1, 0, bl)
    pass_on(0, 0, bl)
    for d in range(NZ * NY):
        peer = ((z + d // NY) % NZ) * NY + (y + d) % NY
        line = for_owner([series[orders[s, peer]] for s in range(CAP)])
        if d == 0:
            partials[ma] = line
        else:
            leaving[d - 1] = line
            send(leaving.at[d - 1], partials.at[ma], p_send, p_recv, bl, peer)

    def cross_near(t):
        half = crossed.at[left // 2, t, pl.ds(0, NY // 2)]
        await_bytes(half, k_recv.at[t, 0])
        send(half, half, k_send, k_recv.at[t, 2], right, ma)
        half = crossed.at[right // 2, t, pl.ds(NY // 2, NY // 2)]
        await_bytes(half, k_recv.at[t, 1])
        send(half, half, k_send, k_recv.at[t, 2], left, ma)
        await_bytes(half, k_recv.at[t, 3])
        pass_on(t, 1, left)
        await_bytes(half, k_recv.at[t, 4])
        pass_on(t, 2, right)

    def cross_far(t):
        await_bytes(crossed.at[across // 2, t], k_recv.at[t, 2])
        pass_on(t, 3, across)

    def view(t, who, first=0, count=CAP):
        return held.at[(z + row[t]) % NZ, who, pl.ds(first, count)]

    def to_sibling(t, who):
        ref = view(t, who)
        send(ref, ref, c_send, c_recv, sibling, ma)

    def keep(t, who, blocks):
        stacked = jnp.concatenate(blocks, axis=0)
        held[(z + row[t]) % NZ, who] = stacked.T.reshape(CAP, ROWS, NY * DEG)

    def collect(t, n, who):
        await_bytes(lined.at[t, 0, pl.ds(0, NY if t else NY - 1)], l_recv.at[t, n])
        if t == 0:
            lined[t, who // 2, y] = crossed[who // 2, t, y]
        keep(t, who, [lined[t, who // 2, j] for j in range(NY)])
        to_sibling(t, who)

    def own_part(t):
        await_bytes(arrived.at[pl.ds(0, NY)], a_recv.at[t - 2])
        at_z = (z + row[t]) % NZ
        keep(t, bl, [arrived[at_z * NY + j] for j in range(NY)])
        lower, upper = (view(t, bl, h * (CAP // 2), CAP // 2) for h in range(2))
        send(lower, lower, x_send, x_recv.at[t - 2, 0], right, ma)
        send(upper, upper, x_send, x_recv.at[t - 2, 1], left, ma)
        send(upper, upper, x_send, x_recv.at[t - 2, 3], right, ma)
        send(lower, lower, x_send, x_recv.at[t - 2, 4], left, ma)
        to_sibling(t, bl)

    def near_part(t):
        half = view(t, left, 0, CAP // 2)
        await_bytes(half, x_recv.at[t - 2, 0])
        send(half, half, x_send, x_recv.at[t - 2, 2], right, ma)
        half = view(t, right, CAP // 2, CAP // 2)
        await_bytes(half, x_recv.at[t - 2, 1])
        send(half, half, x_send, x_recv.at[t - 2, 2], left, ma)
        await_bytes(half, x_recv.at[t - 2, 3])
        to_sibling(t, left)
        await_bytes(half, x_recv.at[t - 2, 4])
        to_sibling(t, right)

    def far_part(t):
        await_bytes(view(t, across), x_recv.at[t - 2, 2])
        to_sibling(t, across)

    cross_near(1)
    cross_near(0)
    own_part(2)
    own_part(3)
    cross_far(1)
    cross_far(0)
    collect(1, 0, bl)
    collect(0, 0, bl)
    near_part(2)
    collect(1, 1, left)
    collect(1, 2, right)
    near_part(3)
    collect(0, 1, left)
    collect(0, 2, right)
    await_bytes(leaving, p_recv)
    line = jnp.sum(partials[...], axis=0)[0:1].astype(BF16).astype(F32)
    spectra[bl] = jnp.broadcast_to(line, (8, 128))
    for d in range(1, 2 * NX):
        send(spectra.at[bl], spectra.at[bl], s_send, s_recv, (bl + d) % (2 * NX), ma)

    collect(1, 3, across)
    far_part(2)
    collect(0, 3, across)
    far_part(3)

    await_bytes(held.at[pl.ds(0, NZ // 2)], c_recv)
    await_bytes(spectra.at[pl.ds(0, 2 * NX - 1)], s_recv)
    await_bytes(crossed.at[pl.ds(0, NX - 1)], k_send)
    await_bytes(outgoing, a_send)
    await_bytes(leaving, p_send)
    await_bytes(crossed.at[pl.ds(0, NX - 1), 0], l_send.at[0])
    await_bytes(crossed.at[:, 1], l_send.at[1])
    await_bytes(held.at[0, pl.ds(0, NX + 2)], x_send)
    await_bytes(held.at[pl.ds(0, NZ // 2)], c_send)
    await_bytes(spectra.at[pl.ds(0, 2 * NX - 1)], s_send)


def gather(orders, legendre, beam, visibility):
    hbm = pl.BlockSpec(memory_space=pltpu.HBM)
    vmem = pl.BlockSpec(memory_space=pltpu.VMEM)
    dma = pltpu.SemaphoreType.DMA
    return pl.pallas_call(
        gather_kernel,
        out_shape=(
            jax.ShapeDtypeStruct((NZ, 2 * NX, CAP, ROWS, NY * DEG), BF16),
            jax.ShapeDtypeStruct((2 * NX, 8, 128), F32),
        ),
        in_specs=[
            hbm,
            hbm,
            hbm,
            hbm,
        ],
        out_specs=(vmem, vmem),
        scratch_shapes=[
            pltpu.SMEM(orders.shape, jnp.int32),
            pltpu.VMEM(legendre.shape, BF16),
            pltpu.VMEM(beam.shape, BF16),
            pltpu.VMEM(visibility.shape, F32),
            pltpu.VMEM((GROUP, ORDERS // GROUP * DEG, GROUP * ROWS), BF16),
            pltpu.VMEM((ORDERS + 1, DEG, 128), BF16),
            pltpu.VMEM((2 * NY, DEG, 128), BF16),
            pltpu.VMEM((NZ * NY, DEG, 128), BF16),
            pltpu.VMEM((NX, 2, NY, DEG, 128), BF16),
            pltpu.VMEM((2, NX, NY, DEG, 128), BF16),
            pltpu.VMEM((ORDERS + 1, 8, 128), F32),
            pltpu.VMEM((NZ * NY - 1, 8, 128), F32),
            pltpu.VMEM((NZ * NY, 8, 128), F32),
            dma((ORDERS // GROUP,)),
            dma((ORDERS // GROUP,)),
            dma((2,)),
            dma,
            dma((2,)),
            dma,
            dma((2, 5)),
            dma((2,)),
            dma((2, 4)),
            dma,
            dma,
            dma,
            dma((2, 5)),
            dma,
            dma,
            dma,
            dma,
        ],
        compiler_params=pltpu.CompilerParams(
            collective_id=0, has_side_effects=True, vmem_limit_bytes=40 * 1024 * 1024
        ),
        name="gather_blocks",
    )(orders, legendre, beam, visibility)


def normal_kernel(blocks_ref, spectra_ref, normal_ref, map_ref, own, turned, result, maps, out_sem):
    bl = lax.axis_index("bl")
    start = pl.multiple_of((bl % 2) * 128, 128)
    skip = pl.multiple_of((bl % 2) * 64, 16)
    scale = 1.0 / 128.0
    width = NY * DEG
    copies = []

    def prepare(s):
        window = blocks_ref[bl // 2, :, s, :, pl.ds(start, 256)].reshape(2 * NX * ROWS, 256)
        pieces = []
        for k in range(2 * NX):
            pieces.append(-window[k * ROWS + ROWS // 2 : (k + 1) * ROWS])
            pieces.append(window[k * ROWS : k * ROWS + ROWS // 2])
        own[s] = window.T
        turned[s] = jnp.concatenate(pieces, axis=0).T

    for s in range(CAP):
        prepare(s)
        left = jnp.concatenate([own[s, pl.ds(skip, 192), :], turned[s, pl.ds(skip, 192), :]], axis=0)
        for n in range(0, NZ, 2):
            right = jnp.concatenate(
                [blocks_ref[n + h, :, s].reshape(2 * NX * ROWS, width) for h in range(2)], axis=1
            )
            product = jnp.dot(left, right, preferred_element_type=F32) * scale
            part = pl.ds(n * width, 2 * width)
            result[s, 0, :, part] = product[0:192].astype(BF16)
            result[s, 1, :, part] = product[192:384].astype(BF16)
            copy = pltpu.make_async_copy(
                result.at[s, :, :, part], normal_ref.at[s, :, :, part], out_sem.at[s * (NZ // 2) + n // 2]
            )
            copy.start()
            copies.append(copy)
    lane = lax.broadcasted_iota(jnp.int32, (8, 128), 1) // ROWS
    for s in range(CAP):
        left = jnp.concatenate([own[s, pl.ds(skip, 192), :], turned[s, pl.ds(skip, 192), :]], axis=0)
        halves = []
        for h in range(2):
            line = jnp.zeros((8, 128), F32)
            for q in range(4):
                moved = pltpu.roll(spectra_ref[h * 4 + q], (q * ROWS + 128 - s * ROWS) % 128, 1)
                line = jnp.where(lane == q, moved, line)
            halves.append(line)
        spectrum = jnp.concatenate(halves, axis=1).astype(BF16)
        adjoint = lax.dot_general(spectrum, left, (((1,), (1,)), ((), ())), preferred_element_type=F32)
        adjoint = adjoint * (1.0 / math.sqrt(128.0))
        maps[s, 0:1, :] = adjoint[0:1, 0:192]
        maps[s, 1:2, :] = adjoint[0:1, 192:384]
    copy = pltpu.make_async_copy(maps, map_ref, out_sem.at[CAP * NZ // 2])
    copy.start()
    copies.append(copy)
    for copy in copies:
        copy.wait()


def normal_maps(blocks, spectra):
    hbm = pl.BlockSpec(memory_space=pltpu.HBM)
    vmem = pl.BlockSpec(memory_space=pltpu.VMEM)
    return pl.pallas_call(
        normal_kernel,
        out_shape=(
            jax.ShapeDtypeStruct((CAP, 2, 192, COLS), BF16),
            jax.ShapeDtypeStruct((CAP, 2, 192), F32),
        ),
        in_specs=[vmem, vmem],
        out_specs=(hbm, hbm),
        scratch_shapes=[
            pltpu.VMEM((CAP, 256, 256), BF16),
            pltpu.VMEM((CAP, 256, 256), BF16),
            pltpu.VMEM((CAP, 2, 192, COLS), BF16),
            pltpu.VMEM((CAP, 2, 192), F32),
            pltpu.SemaphoreType.DMA((CAP * NZ // 2 + 1,)),
        ],
        compiler_params=pltpu.CompilerParams(vmem_limit_bytes=40 * 1024 * 1024),
        name="normal_maps",
    )(blocks, spectra)


def on_device(beam_fringe_harmonics, legendre, visibility, owner_orders):
    in_hbm = [
        pltpu.with_memory_space_constraint(a, pltpu.HBM)
        for a in (owner_orders.T, legendre, beam_fringe_harmonics, visibility)
    ]
    blocks, spectra = gather(*in_hbm)
    return normal_maps(blocks, spectra)


def solution(mesh):
    return jax.shard_map(
        on_device,
        mesh=mesh,
        in_specs=(P("bl", None, None, None), P(None, "ma", None), P("bl", None, "ma"), P()),
        out_specs=(P("ma", None, "bl", None), P("ma", None, "bl")),
        check_vma=False,
    )
```
